32 devices in a mesh: dp: 8 (over y, x, core), mp: 4 (over z).
Axes of the slice: x: 2, y: 2, z: 4, core: 2. Of those that a mesh axis runs over, the one named last changes fastest.
Arguments:
- queries: bfloat16 [1024, 4096], P('dp', 'mp'), may hold values from -100 to 100
- neighbours: bfloat16 [128, 64, 896], P(None, 'dp'), may hold values from -6 to 6
- targets: int32 [64], P('dp'), may hold values from 0 to 31, as said below
- counts: int32 [8], P('dp'), may hold values from 0 to 8, as said below
- in_weight: bfloat16 [896, 3584], P(None, 'mp'), may hold values from -0.1875 to 0.1875
- out_weight: bfloat16 [3584, 896], P('mp'), may hold values from -0.09375 to 0.09375
- kv_weight: bfloat16 [896, 2, 4096], P(None, None, 'mp'), may hold values from -0.1875 to 0.1875
- d_context: bfloat16 [1024, 4096], P('dp', 'mp'), may hold values from -6 to 6
Outputs:
- context: bfloat16 [1024, 4096], P('dp', 'mp')
- d_queries: bfloat16 [1024, 4096], P('dp', 'mp')
- grad_kv: float32 [896, 2, 4096], P('dp', None, 'mp')
- grad_in: float32 [896, 3584], P('dp', 'mp')
- grad_out: float32 [3584, 896], P('mp', 'dp')
The draws below stay inside these ranges and needn't reach their ends.
Inputs may be any that keep to these rules, and one draw needn't show every extreme that they name: Every block index o * 4 + p (o an owner, p < 4) is the target of exactly one live slot over all holders; at most 1 live slots of one holder target one owner, and some holder reaches 1; targets of slots that are not live are arbitrary. counts sum to 4 times the number of devices along dp.
All inputs are finite; a program needn't handle non-finite values.
Results may differ from the reference program's by a relative error of at most 0.04.
Values may be sent and summed in bfloat16 or wider, within the bound.
A program may use at most 64 MiB of HBM per device.

```python
import jax
import jax.numpy as jnp
from jax import lax

H = 32
DH = 128
DE = 896
FE = 3584
SPAN = 64
NLEN = 128
CH = 2
HDH = 4096
NB = 4
HOLD = 8
SLOTS = 64
TOKENS = 1024
N_DP = 8
N_MP = 4


def holder_table(key):
    key_order, key_spread, key_owner, key_place, key_dead = jax.random.split(key, 5)
    holder_order = jax.random.permutation(key_order, N_DP)
    spreads = jax.random.randint(key_spread, (N_DP // 2,), 0, NB + 1)
    spreads = spreads.at[0].set(NB)
    first_half = holder_order[0::2]
    second_half = holder_order[1::2]
    load_counts = jnp.zeros((N_DP,), jnp.int32).at[first_half].set(NB + spreads).at[second_half].set(NB - spreads)
    ordered = load_counts[holder_order]
    ordered_starts = jnp.cumsum(ordered) - ordered
    starts = jnp.zeros((N_DP,), jnp.int32).at[holder_order].set(ordered_starts)
    owner_order = jax.random.permutation(key_owner, N_DP)

    def per_owner(owner_key):
        return jax.random.permutation(owner_key, NB)
    position_table = jax.vmap(per_owner)(jax.random.split(key_place, N_DP))
    slot_index = jnp.arange(HOLD, dtype=jnp.int32)
    entry_index = (starts[:, None] + slot_index[None, :]) % (N_DP * NB)
    owner_ids = owner_order[entry_index % N_DP]
    cycle_index = entry_index // N_DP
    position = position_table[owner_ids, cycle_index]
    is_live = slot_index[None, :] < load_counts[:, None]
    dead_targets = jax.random.randint(key_dead, (N_DP, HOLD), 0, N_DP * NB)
    targets = jnp.where(is_live, owner_ids * NB + position, dead_targets)
    return (targets.reshape(-1).astype(jnp.int32), load_counts.astype(jnp.int32))


def draw_targets(key, part):
    targets, load_counts = holder_table(key)
    return targets


def draw_counts(key, part):
    targets, load_counts = holder_table(key)
    return load_counts


def draw_queries(key, part):
    key = jax.random.fold_in(key, 11)
    key_base = jax.random.fold_in(key, 0)
    values = jnp.clip(jax.random.normal(key_base, (TOKENS, HDH), jnp.float32), -6.0, 6.0)
    return values.astype(jnp.bfloat16)


def steps_of(rng, dims, cuts, smallest, largest):
    level = 1.0
    for dim, parts in cuts:
        draws = jax.random.uniform(jax.random.fold_in(jax.random.fold_in(rng, 6), dim), (parts,), jnp.float32, smallest / len(cuts), largest / len(cuts))
        level = level * jnp.repeat(jnp.exp(draws), dims[dim] // parts).reshape((-1,) + (1,) * (len(dims) - 1 - dim))
    return level


def scatter_about(own_key, shape, deviation, reach, shards=(), kind=jnp.bfloat16):
    entries = jax.random.normal(own_key, shape, jnp.float32) * deviation
    if len(shards) > 0:
        entries = steps_of(own_key, shape, shards, -0.22, 0.18) * entries
    return jnp.clip(entries, min=-reach, max=reach).astype(kind)


def setup_inputs(seed: int = 0) -> dict:
    key_list = jax.random.split(jax.random.key(seed), 9)
    return {
        "queries": draw_queries(jax.random.fold_in(key_list[8], 71), 0),
        "neighbours": scatter_about(key_list[1], (NLEN, SLOTS, DE), 1.0, 6.0, ((1, 8),)),
        "targets": draw_targets(jax.random.fold_in(key_list[8], 71), 0),
        "counts": draw_counts(jax.random.fold_in(key_list[8], 71), 0),
        "in_weight": scatter_about(key_list[4], (DE, FE), DE ** -0.5, 0.1875, ((1, 4),)),
        "out_weight": scatter_about(key_list[5], (FE, DE), FE ** -0.5, 0.09375, ((0, 4),)),
        "kv_weight": scatter_about(key_list[6], (DE, 2, HDH), DE ** -0.5, 0.1875, ((2, 4),)),
        "d_context": scatter_about(key_list[7], (TOKENS, HDH), 1.0, 6.0, ((0, 8), (1, 4))),
    }


GELU_C = 0.7978845608028654
GELU_A = 0.044715
EPSILON = 1e-06

def gelu_value(values):
    inner = GELU_C * (values + GELU_A * values * values * values)
    return 0.5 * values * (1.0 + jnp.tanh(inner))

def gelu_slope(values):
    inner = GELU_C * (values + GELU_A * values * values * values)
    tanh_value = jnp.tanh(inner)
    return 0.5 * (1.0 + tanh_value) + 0.5 * values * (1.0 - tanh_value * tanh_value) * GELU_C * (1.0 + 3.0 * GELU_A * values * values)

def rms_normed(rows):
    wide = rows.astype(jnp.float32)
    mean_square = lax.optimization_barrier(jnp.mean(wide * wide, axis=-1, keepdims=True))
    return (wide * lax.rsqrt(mean_square + EPSILON)).astype(jnp.bfloat16)

def to_spans(values, spans):
    length, blocks, columns = values.shape
    heads = columns // DH
    return values.reshape(length, spans, 2, heads, DH).transpose(1, 2, 0, 3, 4).reshape(spans, 2 * length, heads, DH)

def from_spans(values, length):
    spans, keys_len, heads, depth = values.shape
    return values.reshape(spans, 2, length, heads, depth).transpose(2, 0, 1, 3, 4).reshape(length, 2 * spans, heads * depth)

def attend(queries, keys, values, grads):
    scaling = DH ** (-0.5)
    queries_f = queries.astype(jnp.float32)
    keys_f = keys.astype(jnp.float32)
    values_f = values.astype(jnp.float32)
    grads_f = grads.astype(jnp.float32)
    scores = jnp.einsum('cqhd,ckhd->chqk', queries_f, keys_f) * scaling
    peak = lax.optimization_barrier(jnp.max(scores, axis=-1, keepdims=True))
    weights = jnp.exp(scores - peak)
    probs_wide = weights / lax.optimization_barrier(jnp.sum(weights, axis=-1, keepdims=True))
    probs = probs_wide.astype(jnp.bfloat16)
    context = jnp.einsum('chqk,ckhd->cqhd', probs.astype(jnp.float32), values_f).astype(jnp.bfloat16)
    d_probs = jnp.einsum('cqhd,ckhd->chqk', grads_f, values_f)
    d_scores = (probs_wide * (d_probs - lax.optimization_barrier(jnp.sum(d_probs * probs_wide, axis=-1, keepdims=True))) * scaling).astype(jnp.bfloat16)
    d_scores_f = d_scores.astype(jnp.float32)
    d_queries = jnp.einsum('chqk,ckhd->cqhd', d_scores_f, keys_f).astype(jnp.bfloat16)
    d_keys = jnp.einsum('chqk,cqhd->ckhd', d_scores_f, queries_f).astype(jnp.bfloat16)
    d_values = jnp.einsum('chqk,cqhd->ckhd', probs.astype(jnp.float32), grads_f).astype(jnp.bfloat16)
    return (context, d_queries, d_keys, d_values)

def reference(queries, neighbours, targets, counts, in_weight, out_weight, kv_weight, d_context):
    slot_ids = jnp.arange(SLOTS, dtype=jnp.int32)
    is_live = slot_ids % HOLD < counts[slot_ids // HOLD]
    landing = jnp.where(is_live, targets, N_DP * NB).astype(jnp.int32)
    source = jnp.zeros((N_DP * NB + 1,), jnp.int32).at[landing].set(slot_ids)[:N_DP * NB]
    raw_all = jnp.take(neighbours, source, axis=1).reshape(NLEN, N_DP, NB, DE).transpose(1, 0, 2, 3)
    queries_all = queries.reshape(N_DP, CH * SPAN, HDH)
    grads_all = d_context.reshape(N_DP, CH * SPAN, HDH)
    fe_block = FE // N_MP
    hd_block = HDH // N_MP
    out_blocks = out_weight.astype(jnp.float32).reshape(N_MP, fe_block, DE)
    kv_blocks = kv_weight.astype(jnp.float32).reshape(DE, 2, N_MP, hd_block)

    def owner_step(carry, inputs):
        in_total, out_total, kv_total = carry
        raw, owner_queries, owner_grads = inputs
        normed = rms_normed(raw).reshape(NLEN * NB, DE)
        hidden_pre = jnp.dot(normed, in_weight, preferred_element_type=jnp.float32)
        activated = gelu_value(hidden_pre).astype(jnp.bfloat16)
        partials = jnp.einsum('nmf,mfe->nme', activated.astype(jnp.float32).reshape(NLEN * NB, N_MP, fe_block), out_blocks)
        partials = lax.optimization_barrier(partials.astype(jnp.bfloat16)).astype(jnp.float32)
        encoded = (raw.astype(jnp.float32).reshape(NLEN * NB, DE) + lax.optimization_barrier(jnp.sum(partials, axis=1))).astype(jnp.bfloat16)
        keyvals = jnp.einsum('ne,ejx->njx', encoded.astype(jnp.float32), kv_weight.astype(jnp.float32)).astype(jnp.bfloat16)
        keyvals = keyvals.reshape(NLEN, NB, 2, HDH)
        heads_queries = owner_queries.reshape(CH, SPAN, H, DH)
        heads_grads = owner_grads.reshape(CH, SPAN, H, DH)
        context, d_queries, d_keys, d_values = attend(heads_queries, to_spans(keyvals[:, :, 0], CH), to_spans(keyvals[:, :, 1], CH), heads_grads)
        d_keyvals = jnp.stack([from_spans(d_keys, NLEN), from_spans(d_values, NLEN)], axis=2)
        flat_dkv = d_keyvals.reshape(NLEN * NB, 2, N_MP, hd_block).astype(jnp.float32)
        back_parts = jnp.einsum('njmx,ejmx->nme', flat_dkv, kv_blocks)
        back_parts = lax.optimization_barrier(back_parts.astype(jnp.bfloat16)).astype(jnp.float32)
        d_encoded = lax.optimization_barrier(jnp.sum(back_parts, axis=1)).astype(jnp.bfloat16)
        kv_total = kv_total + jnp.einsum('ne,njx->ejx', encoded.astype(jnp.float32), d_keyvals.reshape(NLEN * NB, 2, HDH).astype(jnp.float32))
        d_act = jnp.dot(d_encoded, out_weight.T, preferred_element_type=jnp.float32)
        d_pre = (d_act * gelu_slope(hidden_pre)).astype(jnp.bfloat16)
        in_total = in_total + jnp.dot(normed.T, d_pre, preferred_element_type=jnp.float32)
        out_total = out_total + jnp.dot(activated.T, d_encoded, preferred_element_type=jnp.float32)
        return ((in_total, out_total, kv_total), (context.reshape(CH * SPAN, HDH), d_queries.reshape(CH * SPAN, HDH)))
    start = (jnp.zeros((DE, FE), jnp.float32), jnp.zeros((FE, DE), jnp.float32), jnp.zeros((DE, 2, HDH), jnp.float32))
    totals, outputs = lax.scan(owner_step, start, (raw_all, queries_all, grads_all))
    grad_in, grad_out, grad_kv = totals
    context_all, d_queries_all = outputs
    return (context_all.reshape(TOKENS, HDH), d_queries_all.reshape(TOKENS, HDH), grad_kv, grad_in, grad_out)
```

```python
import functools

import jax
import jax.numpy as jnp
from jax import lax
from jax.experimental import pallas as pl
from jax.experimental.pallas import tpu as pltpu
from jax.sharding import PartitionSpec as P

DH = 128
SPAN = 64
NEIGH = 2
TAG_ROWS = 16
VMEM_BYTES = 40 * 1024 * 1024


GELU_C = 0.7978845608028654
GELU_A = 0.044715
EPSILON = 1e-06

WHOLE = pl.BlockSpec(memory_space=pltpu.VMEM)


def gelu_value(values):
    inner = GELU_C * (values + GELU_A * values * values * values)
    return 0.5 * values * (1.0 + jnp.tanh(inner))


def gelu_slope(values):
    inner = GELU_C * (values + GELU_A * values * values * values)
    tanh_value = jnp.tanh(inner)
    return 0.5 * (1.0 + tanh_value) + 0.5 * values * (1.0 - tanh_value * tanh_value) * GELU_C * (
        1.0 + 3.0 * GELU_A * values * values
    )


def rms_normed(rows):
    wide = rows.astype(jnp.float32)
    mean_square = jnp.mean(wide * wide, axis=-1, keepdims=True)
    return (wide * lax.rsqrt(mean_square + EPSILON)).astype(jnp.bfloat16)


def ring_peer(axis, step):
    size = lax.axis_size(axis)
    return {axis: lax.rem(lax.axis_index(axis) + step, size)}


def flip_partner(bit):
    me = lax.axis_index("dp")
    mine = lax.rem(lax.div(me, 1 << bit), 2)
    return {"dp": me + (1 - 2 * mine) * (1 << bit)}, mine


def greet(peers):
    barrier = pltpu.get_barrier_semaphore()
    for peer in peers:
        pl.semaphore_signal(barrier, inc=1, device_id=peer, device_id_type=pl.DeviceIdType.MESH)
    pl.semaphore_wait(barrier, len(peers))


def remote(src, dst, send_sem, recv_sem, peer):
    return pltpu.make_async_remote_copy(
        src_ref=src,
        dst_ref=dst,
        send_sem=send_sem,
        recv_sem=recv_sem,
        device_id=peer,
        device_id_type=pl.DeviceIdType.MESH,
    )


class SumOverMp:
    def __init__(self, size, part, raw, out, landing, sems):
        self.size, self.part, self.raw, self.out, self.landing = size, part, raw, out, landing
        self.send1, self.recv1, self.send2, self.recv2 = sems
        self.me = lax.axis_index("mp")

    def scatter(self, step):
        peer = ring_peer("mp", step)
        return remote(
            self.part.at[peer["mp"]],
            self.landing.at[step - 1],
            self.send1.at[step - 1],
            self.recv1.at[step - 1],
            peer,
        )

    def gather(self, step):
        return remote(
            self.out.at[self.me],
            self.out.at[self.me],
            self.send2.at[step - 1],
            self.recv2.at[step - 1],
            ring_peer("mp", step),
        )

    def begin(self):
        for step in range(1, self.size):
            self.scatter(step).start()

    def reduce(self):
        total = self.part[self.me].astype(jnp.float32)
        for step in range(1, self.size):
            self.scatter(step).wait_recv()
            total = total + self.landing[step - 1].astype(jnp.float32)
        if self.raw is not None:
            total = total + self.raw[self.me].astype(jnp.float32)
        self.out[self.me] = total.astype(jnp.bfloat16)
        for step in range(1, self.size):
            self.gather(step).start()

    def finish(self):
        for step in range(1, self.size):
            self.gather(step).wait_recv()
        for step in range(1, self.size):
            self.scatter(step).wait_send()
            self.gather(step).wait_send()


class HalvingOverDp:
    def __init__(self, bits, source, out, buffers, sends, recvs):
        self.bits, self.source, self.out, self.buffers = bits, source, out, buffers
        self.sends, self.recvs = sends, recvs
        self.flips = [flip_partner(bit) for bit in bits]
        self.stages = len(bits)

    def held(self, stage, group, low):
        if stage > 0:
            return self.buffers[stage - 1].at[2 * group + low]
        rest = sum(((group >> s) & 1) << bit for s, bit in enumerate(self.bits[1:]))
        return self.source.at[rest + low * (1 << self.bits[0])]

    def held_dynamic(self, stage, group_base, group_low, low):
        if stage > 0:
            return self.buffers[stage - 1].at[2 * (2 * group_base + group_low) + low]
        rest = sum(((group_base >> s) & 1) << bit for s, bit in enumerate(self.bits[2:]))
        return self.source.at[rest + group_low * (1 << self.bits[1]) + low * (1 << self.bits[0])]

    def copy(self, stage, group, group_low):
        peer, mine = self.flips[stage]
        if stage == self.stages - 1:
            src, slot = self.held(stage, group, 1 - mine), group
        else:
            src = self.held_dynamic(stage, group, group_low, 1 - mine)
            slot = 2 * group + group_low
        return remote(
            src,
            self.buffers[stage].at[slot],
            self.sends[stage].at[slot],
            self.recvs[stage].at[slot],
            peer,
        )

    def orders(self, stage):
        if stage == self.stages - 1:
            return [(0, 0)]
        next_mine = self.flips[stage + 1][1]
        count = 1 << (self.stages - stage - 2)
        return [(g, 1 - next_mine) for g in range(count)] + [(g, next_mine) for g in range(count)]

    def begin(self):
        for group, low in self.orders(0):
            self.copy(0, group, low).start()

    def step(self, stage):
        mine = self.flips[stage][1]
        orders = self.orders(stage)
        ahead = self.orders(stage + 1)
        count = len(orders) // 2
        buffer = self.buffers[stage]
        for place, (group, low) in enumerate(orders):
            self.copy(stage, group, low).wait_recv()
            slot = 2 * group + low
            kept = self.held_dynamic(stage, group, low, mine)[...].astype(jnp.float32)
            buffer[slot] = (kept + buffer[slot].astype(jnp.float32)).astype(jnp.bfloat16)
            if place == count - 1:
                for next_group, next_low in ahead:
                    self.copy(stage + 1, next_group, next_low).start()

    def last(self):
        stage = self.stages - 1
        mine = self.flips[stage][1]
        self.copy(stage, 0, 0).wait_recv()
        kept = self.held(stage, 0, mine)[...].astype(jnp.float32)
        self.out[...] = kept + self.buffers[stage][0].astype(jnp.float32)

    def finish(self):
        for stage in range(self.stages):
            for group, low in self.orders(stage):
                self.copy(stage, group, low).wait_send()


def dp_bits(count):
    total = count.bit_length() - 1
    forward = list(range(total))
    return forward, forward[:1] + forward[:0:-1]


def halving_scratch(count, chunk):
    stages = count.bit_length() - 1
    sizes = [count >> (stage + 1) for stage in range(stages)]
    return (
        [pltpu.VMEM((size,) + chunk, jnp.bfloat16) for size in sizes]
        + [pltpu.SemaphoreType.DMA((size,)) for size in sizes]
        + [pltpu.SemaphoreType.DMA((size,)) for size in sizes]
    )


def halving_of(bits, source, out, scratch):
    stages = len(bits)
    return HalvingOverDp(
        bits, source, out, scratch[:stages], scratch[stages : 2 * stages], scratch[2 * stages :]
    )


def mp_scratch(size, rows, width):
    return [pltpu.VMEM((size - 1, rows, width), jnp.bfloat16)] + [
        pltpu.SemaphoreType.DMA((size - 1,)) for _ in range(4)
    ]


def params(collective_id):
    return pltpu.CompilerParams(
        collective_id=collective_id, has_side_effects=True, vmem_limit_bytes=VMEM_BYTES
    )


def mp_peers():
    return [ring_peer("mp", step) for step in range(1, lax.axis_size("mp"))]


def dp_flip_peers(count):
    return [flip_partner(bit)[0] for bit in range(count.bit_length() - 1)]


def route_kernel(n_dp, n_mp, message, out, landing, send1, recv1, send2, recv2):
    greet([ring_peer("dp", step) for step in range(1, n_dp)] + mp_peers())
    blocks = out.shape[0]
    rows = message.shape[1] - TAG_ROWS
    me_dp, me_mp = lax.axis_index("dp"), lax.axis_index("mp")

    def exchange(step):
        peer = ring_peer("dp", step)
        return remote(
            message.at[peer["dp"]],
            landing.at[step - 1],
            send1.at[step - 1],
            recv1.at[step - 1],
            peer,
        )

    for step in range(1, n_dp):
        exchange(step).start()
    data = message[me_dp, :rows].astype(jnp.float32)
    tag = message[me_dp, rows:].astype(jnp.float32)[:1]
    placed = [jnp.where(tag == block + 1.0, data, 0.0) for block in range(blocks)]
    for step in range(1, n_dp):
        exchange(step).wait_recv()
        data = landing[step - 1, :rows].astype(jnp.float32)
        tag = landing[step - 1, rows:].astype(jnp.float32)[:1]
        placed = [
            jnp.where(tag == block + 1.0, data, placed[block]) for block in range(blocks)
        ]
    mine = pl.ds(pl.multiple_of(me_mp * rows, rows), rows)
    for block in range(blocks):
        out[block, mine] = placed[block].astype(jnp.bfloat16)

    def gather(step):
        return remote(
            out.at[:, mine],
            out.at[:, mine],
            send2.at[step - 1],
            recv2.at[step - 1],
            ring_peer("mp", step),
        )

    for step in range(1, n_mp):
        gather(step).start()
    for step in range(1, n_mp):
        gather(step).wait_recv()
    for step in range(1, n_dp):
        exchange(step).wait_send()
    for step in range(1, n_mp):
        gather(step).wait_send()


def route(message, n_dp, n_mp, blocks, length):
    tall, width = message.shape[1:]
    return pl.pallas_call(
        functools.partial(route_kernel, n_dp, n_mp),
        out_shape=jax.ShapeDtypeStruct((blocks, length, width), jnp.bfloat16),
        in_specs=[WHOLE],
        out_specs=WHOLE,
        scratch_shapes=[
            pltpu.VMEM((n_dp - 1, tall, width), jnp.bfloat16),
            pltpu.SemaphoreType.DMA((n_dp - 1,)),
            pltpu.SemaphoreType.DMA((n_dp - 1,)),
            pltpu.SemaphoreType.DMA((n_mp - 1,)),
            pltpu.SemaphoreType.DMA((n_mp - 1,)),
        ],
        compiler_params=params(0),
        name="route",
    )(message)


def sum_kernel(n_mp, part, raw, out, landing, *sems):
    greet(mp_peers())
    total = SumOverMp(n_mp, part, raw, out, landing, sems)
    total.begin()
    total.reduce()
    total.finish()


def sum_over_mp(part, raw, n_mp):
    rows, width = part.shape[1:]
    return pl.pallas_call(
        functools.partial(sum_kernel, n_mp),
        out_shape=jax.ShapeDtypeStruct(part.shape, jnp.bfloat16),
        in_specs=[WHOLE, WHOLE],
        out_specs=WHOLE,
        scratch_shapes=mp_scratch(n_mp, rows, width),
        compiler_params=params(1),
        name="sum_encoded",
    )(part, raw)


def back_kernel(n_mp, n_dp, part, first, second, out, out_first, out_second, landing, *rest):
    greet(mp_peers() + dp_flip_peers(n_dp))
    sems, rest = rest[:4], rest[4:]
    half = len(rest) // 2
    bits = dp_bits(n_dp)
    total = SumOverMp(n_mp, part, None, out, landing, sems)
    pair = [
        halving_of(bits[0], first, out_first, rest[:half]),
        halving_of(bits[1], second, out_second, rest[half:]),
    ]
    total.begin()
    for one in pair:
        one.begin()
    for one in pair:
        one.step(0)
    total.reduce()
    for stage in range(1, len(bits[0]) - 1):
        for one in pair:
            one.step(stage)
    for one in pair:
        one.last()
    total.finish()
    for one in pair:
        one.finish()


def back_sums(part, first, second, n_mp, n_dp):
    rows, width = part.shape[1:]
    chunk = first.shape[1:]
    return pl.pallas_call(
        functools.partial(back_kernel, n_mp, n_dp),
        out_shape=(
            jax.ShapeDtypeStruct(part.shape, jnp.bfloat16),
            jax.ShapeDtypeStruct(chunk, jnp.float32),
            jax.ShapeDtypeStruct(chunk, jnp.float32),
        ),
        in_specs=[WHOLE] * 3,
        out_specs=(WHOLE,) * 3,
        scratch_shapes=mp_scratch(n_mp, rows, width)
        + halving_scratch(n_dp, chunk)
        + halving_scratch(n_dp, chunk),
        compiler_params=params(2),
        name="sum_back",
    )(part, first, second)


def grads_kernel(n_dp, first, second, out_first, out_second, *rest):
    greet(dp_flip_peers(n_dp))
    half = len(rest) // 2
    bits = dp_bits(n_dp)
    pair = [
        halving_of(bits[0], first, out_first, rest[:half]),
        halving_of(bits[1], second, out_second, rest[half:]),
    ]
    for one in pair:
        one.begin()
    for stage in range(len(bits[0]) - 1):
        for one in pair:
            one.step(stage)
    for one in pair:
        one.last()
    for one in pair:
        one.finish()


def grad_sums(first, second, n_dp):
    chunk = first.shape[1:]
    return pl.pallas_call(
        functools.partial(grads_kernel, n_dp),
        out_shape=(
            jax.ShapeDtypeStruct(chunk, jnp.float32),
            jax.ShapeDtypeStruct(chunk, jnp.float32),
        ),
        in_specs=[WHOLE] * 2,
        out_specs=(WHOLE,) * 2,
        scratch_shapes=halving_scratch(n_dp, chunk) + halving_scratch(n_dp, chunk),
        compiler_params=params(3),
        name="sum_grads",
    )(first, second)


def matmul(left, right, left_dim, right_dim):
    return lax.dot_general(
        left, right, (((left_dim,), (right_dim,)), ((), ())), preferred_element_type=jnp.float32
    )


def attend_kernel(spans, queries, keys, values, grads, context, d_queries, d_keys, d_values):
    scaling = DH ** (-0.5)
    wide = keys.shape[0] // spans
    for span in range(spans):
        own = pl.ds(span * SPAN, SPAN)
        seen = pl.ds(span * wide, wide)
        q, g = queries[own, :], grads[own, :]
        k, v = keys[seen, :], values[seen, :]
        scores = matmul(q, k, 1, 1) * scaling
        weights = jnp.exp(scores - jnp.max(scores, axis=-1, keepdims=True))
        probs_wide = weights / jnp.sum(weights, axis=-1, keepdims=True)
        probs = probs_wide.astype(jnp.bfloat16)
        context[own, :] = matmul(probs, v, 1, 0).astype(jnp.bfloat16)
        d_probs = matmul(g, v, 1, 1)
        inner = jnp.sum(d_probs * probs_wide, axis=-1, keepdims=True)
        d_scores = (probs_wide * (d_probs - inner) * scaling).astype(jnp.bfloat16)
        d_queries[own, :] = matmul(d_scores, k, 1, 0).astype(jnp.bfloat16)
        d_keys[seen, :] = matmul(d_scores, q, 0, 0).astype(jnp.bfloat16)
        d_values[seen, :] = matmul(probs, g, 0, 0).astype(jnp.bfloat16)


def attend(queries, keys, values, grads, spans):
    rows, columns = queries.shape
    count = keys.shape[0]
    narrow = pl.BlockSpec((rows, DH), lambda head: (0, head))
    tall = pl.BlockSpec((count, DH), lambda head: (0, head))
    small = jax.ShapeDtypeStruct((rows, columns), jnp.bfloat16)
    large = jax.ShapeDtypeStruct((count, columns), jnp.bfloat16)
    return pl.pallas_call(
        functools.partial(attend_kernel, spans),
        out_shape=(small, small, large, large),
        grid=(columns // DH,),
        in_specs=[narrow, tall, tall, narrow],
        out_specs=(narrow, narrow, tall, tall),
        compiler_params=pltpu.CompilerParams(vmem_limit_bytes=VMEM_BYTES),
        name="attend",
    )(queries, keys, values, grads)


def per_device(queries, neighbours, targets, counts, in_weight, out_weight, kv_weight, d_context):
    length, holding, width = neighbours.shape
    n_dp, n_mp = lax.axis_size("dp"), lax.axis_size("mp")
    slice_rows = length // n_mp
    spans = queries.shape[0] // SPAN
    blocks = NEIGH * spans
    tokens = blocks * length
    is_live = jnp.arange(holding, dtype=jnp.int32) < counts[0]
    owners = jnp.arange(n_dp, dtype=jnp.int32)
    chosen = jnp.logical_and((targets // blocks)[None, :] == owners[:, None], is_live[None, :])
    tags = jnp.sum(jnp.where(chosen, (targets % blocks)[None, :] + 1, 0), axis=1)
    own = lax.dynamic_slice_in_dim(neighbours, lax.axis_index("mp") * slice_rows, slice_rows, 0)
    moved = jnp.einsum(
        "oh,thd->otd", chosen.astype(jnp.bfloat16), own, preferred_element_type=jnp.float32
    ).astype(jnp.bfloat16)
    tag_rows = jnp.broadcast_to(
        tags.astype(jnp.bfloat16)[:, None, None], (n_dp, TAG_ROWS, width)
    )
    message = jnp.concatenate([moved, tag_rows], axis=1)
    raw = route(message, n_dp, n_mp, blocks, length).reshape(tokens, width)

    normed = rms_normed(raw)
    hidden_pre = jnp.dot(normed, in_weight, preferred_element_type=jnp.float32)
    activated = gelu_value(hidden_pre).astype(jnp.bfloat16)
    part = jnp.dot(activated, out_weight, preferred_element_type=jnp.float32).astype(jnp.bfloat16)
    sliced = (n_mp, tokens // n_mp, width)
    encoded = sum_over_mp(part.reshape(sliced), raw.reshape(sliced), n_mp).reshape(tokens, width)

    key_weight, value_weight = kv_weight[:, 0], kv_weight[:, 1]
    keys = jnp.dot(encoded, key_weight, preferred_element_type=jnp.float32).astype(jnp.bfloat16)
    values = jnp.dot(encoded, value_weight, preferred_element_type=jnp.float32).astype(
        jnp.bfloat16
    )
    context, d_queries, d_keys, d_values = attend(queries, keys, values, d_context, spans)

    back = (matmul(d_keys, key_weight, 1, 1) + matmul(d_values, value_weight, 1, 1)).astype(
        jnp.bfloat16
    )
    chunked = (n_dp, width // n_dp, -1)
    key_terms = matmul(encoded, d_keys, 0, 0).astype(jnp.bfloat16).reshape(chunked)
    value_terms = matmul(encoded, d_values, 0, 0).astype(jnp.bfloat16).reshape(chunked)
    d_encoded, grad_key, grad_value = back_sums(
        back.reshape(sliced), key_terms, value_terms, n_mp, n_dp
    )
    d_encoded = d_encoded.reshape(tokens, width)

    d_act = matmul(d_encoded, out_weight, 1, 1)
    d_pre = (d_act * gelu_slope(hidden_pre)).astype(jnp.bfloat16)
    in_terms = matmul(normed, d_pre, 0, 0).astype(jnp.bfloat16).reshape(chunked)
    out_terms = matmul(d_encoded, activated, 0, 0).astype(jnp.bfloat16).reshape(chunked)
    grad_in, grad_out_t = grad_sums(in_terms, out_terms, n_dp)
    return (
        context,
        d_queries,
        jnp.stack([grad_key, grad_value], axis=1),
        grad_in,
        grad_out_t.T,
    )


def solution(mesh):
    placed = (
        P("dp", "mp"),
        P(None, "dp", None),
        P("dp"),
        P("dp"),
        P(None, "mp"),
        P("mp", None),
        P(None, None, "mp"),
        P("dp", "mp"),
    )
    return jax.shard_map(
        per_device,
        mesh=mesh,
        in_specs=placed,
        out_specs=(P("dp", "mp"), P("dp", "mp"), P("dp", None, "mp"), P("dp", "mp"), P("mp", "dp")),
        check_vma=False,
    )
```

```python
import functools

import jax
import jax.numpy as jnp
from jax import lax
from jax.experimental import pallas as pl
from jax.experimental.pallas import tpu as pltpu
from jax.sharding import PartitionSpec as P

DH = 128
SPAN = 64
NEIGH = 2
TAG_ROWS = 16
CHAIN_CHUNKS = 16
CHAIN_LAG = 2
CHAIN_WINDOW = 4
HEADS_AT_ONCE = 2
VMEM_BYTES = 40 * 1024 * 1024


GELU_C = 0.7978845608028654
GELU_A = 0.044715
EPSILON = 1e-06

WHOLE = pl.BlockSpec(memory_space=pltpu.VMEM)


def gelu_value(values):
    inner = GELU_C * (values + GELU_A * values * values * values)
    return 0.5 * values * (1.0 + jnp.tanh(inner))


def gelu_slope(values):
    inner = GELU_C * (values + GELU_A * values * values * values)
    tanh_value = jnp.tanh(inner)
    return 0.5 * (1.0 + tanh_value) + 0.5 * values * (1.0 - tanh_value * tanh_value) * GELU_C * (
        1.0 + 3.0 * GELU_A * values * values
    )


def rms_normed(rows):
    wide = rows.astype(jnp.float32)
    mean_square = jnp.mean(wide * wide, axis=-1, keepdims=True)
    return (wide * lax.rsqrt(mean_square + EPSILON)).astype(jnp.bfloat16)


def ring_peer(axis, step):
    size = lax.axis_size(axis)
    return {axis: lax.rem(lax.axis_index(axis) + step, size)}


def flip_partner(bit):
    me = lax.axis_index("dp")
    mine = lax.rem(lax.div(me, 1 << bit), 2)
    return {"dp": me + (1 - 2 * mine) * (1 << bit)}, mine


def greet(peers):
    barrier = pltpu.get_barrier_semaphore()
    for peer in peers:
        pl.semaphore_signal(barrier, inc=1, device_id=peer, device_id_type=pl.DeviceIdType.MESH)
    pl.semaphore_wait(barrier, len(peers))


def remote(src, dst, send_sem, recv_sem, peer):
    return pltpu.make_async_remote_copy(
        src_ref=src,
        dst_ref=dst,
        send_sem=send_sem,
        recv_sem=recv_sem,
        device_id=peer,
        device_id_type=pl.DeviceIdType.MESH,
    )


class ChainOverMp:
    def __init__(self, size, part, raw, out, scratch):
        self.size, self.part, self.raw, self.out = size, part, raw, out
        self.staged, self.landing, self.up_send, self.up_recv, self.out_send, self.out_recv = scratch
        self.me = lax.axis_index("mp")
        self.chunks = part.shape[0]
        self.is_end = jnp.logical_or(self.me == 0, self.me == size - 1)
        self.steps = self.chunks + CHAIN_LAG

    def root(self, chunk):
        return self.size // 2 - 1 + chunk % 2

    def up(self, chunk, toward, source):
        side = 0 if toward > 0 else 1
        return remote(
            source.at[chunk],
            self.landing.at[side, chunk],
            self.up_send.at[chunk],
            self.up_recv.at[side, chunk],
            {"mp": self.me + toward},
        )

    def outward(self, chunk, toward):
        side = 0 if toward > 0 else 1
        return remote(
            self.out.at[chunk],
            self.out.at[chunk],
            self.out_send.at[side, chunk],
            self.out_recv.at[chunk],
            {"mp": self.me + toward},
        )

    def arrived(self, chunk, toward):
        self.up(chunk, toward, self.staged).wait_recv()
        return self.landing[0 if toward > 0 else 1, chunk].astype(jnp.float32)

    def inner_up(self, chunk):
        root = self.root(chunk)
        own = self.part[chunk].astype(jnp.float32)
        for toward, here in ((1, self.me < root), (-1, self.me > root)):

            @pl.when(here)
            def _(toward=toward):
                total = own + self.arrived(chunk, toward)
                self.staged[chunk] = total.astype(jnp.bfloat16)
                self.up(chunk, toward, self.staged).start()

        @pl.when(self.me == root)
        def _():
            total = own + self.arrived(chunk, 1) + self.arrived(chunk, -1)
            if self.raw is not None:
                total = total + self.raw[chunk].astype(jnp.float32)
            self.out[chunk] = total.astype(jnp.bfloat16)
            self.outward(chunk, 1).start()
            self.outward(chunk, -1).start()

    def inner_down(self, chunk):
        root = self.root(chunk)
        for toward, here in ((-1, self.me < root), (1, self.me > root)):

            @pl.when(here)
            def _(toward=toward):
                self.outward(chunk, toward).wait_recv()
                self.outward(chunk, toward).start()

    def end_up(self, chunk):
        for toward, here in ((1, self.me == 0), (-1, self.me == self.size - 1)):

            @pl.when(here)
            def _(toward=toward):
                if chunk >= CHAIN_WINDOW:
                    self.up(chunk - CHAIN_WINDOW, toward, self.part).wait_send()
                self.up(chunk, toward, self.part).start()

    def step(self, index):
        @pl.when(self.is_end)
        def _():
            if index < self.chunks:
                self.end_up(index)

        @pl.when(jnp.logical_not(self.is_end))
        def _():
            if index < self.chunks:
                self.inner_up(index)
            if index >= CHAIN_LAG:
                self.inner_down(index - CHAIN_LAG)

    def finish(self):
        for toward, here in ((1, self.me == 0), (-1, self.me == self.size - 1)):

            @pl.when(here)
            def _(toward=toward):
                for chunk in range(self.chunks):
                    self.outward(chunk, toward).wait_recv()
                for chunk in range(self.chunks - CHAIN_WINDOW, self.chunks):
                    self.up(chunk, toward, self.part).wait_send()

        @pl.when(jnp.logical_not(self.is_end))
        def _():
            for chunk in range(self.chunks):
                root = self.root(chunk)
                for toward, here in ((1, self.me < root), (-1, self.me > root)):

                    @pl.when(here)
                    def _(toward=toward):
                        self.up(chunk, toward, self.staged).wait_send()
                        self.outward(chunk, -toward).wait_send()

                @pl.when(self.me == root)
                def _():
                    self.outward(chunk, 1).wait_send()
                    self.outward(chunk, -1).wait_send()


class HalvingOverDp:
    def __init__(self, bits, source, out, buffers, sends, recvs):
        self.bits, self.source, self.out, self.buffers = bits, source, out, buffers
        self.sends, self.recvs = sends, recvs
        self.flips = [flip_partner(bit) for bit in bits]
        self.stages = len(bits)

    def held(self, stage, group, low):
        wanted = (low,) + group
        if stage > 0:
            return self.buffers[stage - 1].at[self.slot(wanted)]
        return self.source.at[sum(value * (1 << bit) for value, bit in zip(wanted, self.bits))]

    def slot(self, group):
        return sum((value * (1 << place) for place, value in enumerate(group)), 0)

    def copy(self, stage, group):
        peer, mine = self.flips[stage]
        slot = self.slot(group)
        return remote(
            self.held(stage, group, 1 - mine),
            self.buffers[stage].at[slot],
            self.sends[stage].at[slot],
            self.recvs[stage].at[slot],
            peer,
        )

    def orders(self, stage):
        if stage == self.stages - 1:
            return [()]
        later = self.orders(stage + 1)
        mine = self.flips[stage + 1][1]
        return [(1 - mine,) + group for group in later] + [(mine,) + group for group in later]

    def begin(self):
        for group in self.orders(0):
            self.copy(0, group).start()

    def units(self):
        return [
            functools.partial(self.unit, stage, place)
            for stage in range(self.stages - 1)
            for place in range(len(self.orders(stage)))
        ] + [self.last]

    def unit(self, stage, place):
        mine = self.flips[stage][1]
        orders = self.orders(stage)
        group = orders[place]
        buffer = self.buffers[stage]
        self.copy(stage, group).wait_recv()
        slot = self.slot(group)
        kept = self.held(stage, group, mine)[...].astype(jnp.float32)
        buffer[slot] = (kept + buffer[slot].astype(jnp.float32)).astype(jnp.bfloat16)
        if place < len(orders) // 2:
            self.copy(stage + 1, self.orders(stage + 1)[place]).start()

    def last(self):
        stage = self.stages - 1
        mine = self.flips[stage][1]
        self.copy(stage, ()).wait_recv()
        kept = self.held(stage, (), mine)[...].astype(jnp.float32)
        self.out[...] = kept + self.buffers[stage][0].astype(jnp.float32)

    def finish(self):
        for stage in range(self.stages):
            for group in self.orders(stage):
                self.copy(stage, group).wait_send()


def dp_bits(count):
    total = count.bit_length() - 1
    forward = list(range(total))
    return forward, forward[:1] + forward[:0:-1]


def halving_scratch(count, chunk):
    stages = count.bit_length() - 1
    sizes = [count >> (stage + 1) for stage in range(stages)]
    return (
        [pltpu.VMEM((size,) + chunk, jnp.bfloat16) for size in sizes]
        + [pltpu.SemaphoreType.DMA((size,)) for size in sizes]
        + [pltpu.SemaphoreType.DMA((size,)) for size in sizes]
    )


def halving_of(bits, source, out, scratch):
    stages = len(bits)
    return HalvingOverDp(
        bits, source, out, scratch[:stages], scratch[stages : 2 * stages], scratch[2 * stages :]
    )


def mp_scratch(chunks, rows, width):
    return [
        pltpu.VMEM((chunks, rows, width), jnp.bfloat16),
        pltpu.VMEM((2, chunks, rows, width), jnp.bfloat16),
        pltpu.SemaphoreType.DMA((chunks,)),
        pltpu.SemaphoreType.DMA((2, chunks)),
        pltpu.SemaphoreType.DMA((2, chunks)),
        pltpu.SemaphoreType.DMA((chunks,)),
    ]


def params(collective_id):
    return pltpu.CompilerParams(
        collective_id=collective_id, has_side_effects=True, vmem_limit_bytes=VMEM_BYTES
    )


def mp_peers():
    return [ring_peer("mp", step) for step in range(1, lax.axis_size("mp"))]


def dp_flip_peers(count):
    return [flip_partner(bit)[0] for bit in range(count.bit_length() - 1)]


def route_kernel(n_dp, n_mp, straight, split, *refs):
    if straight:
        message, whole, out, landing, whole_landing, *sems = refs
    else:
        message, out, landing, *sems = refs
    greet([ring_peer("dp", step) for step in range(1, n_dp)] + mp_peers())
    blocks = out.shape[0]
    me_dp, me_mp = lax.axis_index("dp"), lax.axis_index("mp")

    def exchange(source, target, step, send, recv):
        peer = ring_peer("dp", step)
        return remote(
            source.at[peer["dp"]], target.at[step - 1], send.at[step - 1], recv.at[step - 1], peer
        )

    def parts(step):
        return exchange(message, landing, step, sems[0], sems[1])

    def wholes(step):
        return exchange(whole, whole_landing, step, sems[4], sems[5])

    others = range(1, n_dp)
    for step in others:
        parts(step).start()
    if straight:
        for step in others:
            wholes(step).start()

    def tags_of(rows):
        return rows.astype(jnp.float32)[:1]

    for step in others:
        parts(step).wait_recv()
    data_rows = pl.ds(0, split)
    tag_rows = pl.ds(split, TAG_ROWS)
    tags = [tags_of(message[me_dp, tag_rows])] + [
        tags_of(landing[step - 1, tag_rows]) for step in others
    ]

    def place(own, arrived, first, where):
        sources = [own[me_dp, first]] + [arrived[step - 1, first] for step in others]
        sources = [rows.astype(jnp.float32) for rows in sources]
        for block in range(blocks):
            value = jnp.zeros_like(sources[0])
            for tag, rows in zip(tags, sources):
                value = jnp.where(tag == block + 1.0, rows, value)
            out[block, where] = value.astype(jnp.bfloat16)

    mine = pl.ds(pl.multiple_of(straight + me_mp * split, 16), split)
    place(message, landing, data_rows, mine)

    def gather(step):
        return remote(
            out.at[:, mine],
            out.at[:, mine],
            sems[2].at[step - 1],
            sems[3].at[step - 1],
            ring_peer("mp", step),
        )

    for step in range(1, n_mp):
        gather(step).start()
    if straight:
        for step in others:
            wholes(step).wait_recv()
        for first in range(0, straight, 16):
            rows = pl.ds(first, 16)
            place(whole, whole_landing, rows, rows)
    for step in range(1, n_mp):
        gather(step).wait_recv()
    for step in others:
        parts(step).wait_send()
        if straight:
            wholes(step).wait_send()
    for step in range(1, n_mp):
        gather(step).wait_send()


def route(messages, n_dp, n_mp, blocks, length, straight, split):
    width = messages[0].shape[2]
    return pl.pallas_call(
        functools.partial(route_kernel, n_dp, n_mp, straight, split),
        out_shape=jax.ShapeDtypeStruct((blocks, length, width), jnp.bfloat16),
        in_specs=[WHOLE] * len(messages),
        out_specs=WHOLE,
        scratch_shapes=[
            pltpu.VMEM((n_dp - 1,) + message.shape[1:], jnp.bfloat16) for message in messages
        ]
        + [
            pltpu.SemaphoreType.DMA((n_dp - 1,)),
            pltpu.SemaphoreType.DMA((n_dp - 1,)),
            pltpu.SemaphoreType.DMA((n_mp - 1,)),
            pltpu.SemaphoreType.DMA((n_mp - 1,)),
            pltpu.SemaphoreType.DMA((n_dp - 1,)),
            pltpu.SemaphoreType.DMA((n_dp - 1,)),
        ],
        compiler_params=params(0),
        name="route",
    )(*messages)


def sum_kernel(n_mp, part, raw, out, *scratch):
    greet(mp_peers())
    total = ChainOverMp(n_mp, part, raw, out, scratch)
    for index in range(total.steps):
        total.step(index)
    total.finish()


def sum_over_mp(part, raw, n_mp):
    rows, width = part.shape[1:]
    return pl.pallas_call(
        functools.partial(sum_kernel, n_mp),
        out_shape=jax.ShapeDtypeStruct(part.shape, jnp.bfloat16),
        in_specs=[WHOLE, WHOLE],
        out_specs=WHOLE,
        scratch_shapes=mp_scratch(part.shape[0], rows, width),
        compiler_params=params(1),
        name="sum_encoded",
    )(part, raw)


def interleaved(pair):
    return [unit for both in zip(*(one.units() for one in pair)) for unit in both]


def back_kernel(n_mp, n_dp, part, first, second, out, out_first, out_second, *rest):
    greet(mp_peers() + dp_flip_peers(n_dp))
    chain, rest = rest[:6], rest[6:]
    half = len(rest) // 2
    bits = dp_bits(n_dp)
    total = ChainOverMp(n_mp, part, None, out, chain)
    pair = [
        halving_of(bits[0], first, out_first, rest[:half]),
        halving_of(bits[1], second, out_second, rest[half:]),
    ]
    for one in pair:
        one.begin()
    units = interleaved(pair)
    for index in range(total.steps):
        total.step(index)
        if index > 0 and units:
            units.pop(0)()
    for unit in units:
        unit()
    total.finish()
    for one in pair:
        one.finish()


def back_sums(part, first, second, n_mp, n_dp):
    rows, width = part.shape[1:]
    chunk = first.shape[1:]
    return pl.pallas_call(
        functools.partial(back_kernel, n_mp, n_dp),
        out_shape=(
            jax.ShapeDtypeStruct(part.shape, jnp.bfloat16),
            jax.ShapeDtypeStruct(chunk, jnp.float32),
            jax.ShapeDtypeStruct(chunk, jnp.float32),
        ),
        in_specs=[WHOLE] * 3,
        out_specs=(WHOLE,) * 3,
        scratch_shapes=mp_scratch(part.shape[0], rows, width)
        + halving_scratch(n_dp, chunk)
        + halving_scratch(n_dp, chunk),
        compiler_params=params(2),
        name="sum_back",
    )(part, first, second)


def grads_kernel(n_dp, first, second, out_first, out_second, *rest):
    greet(dp_flip_peers(n_dp))
    half = len(rest) // 2
    bits = dp_bits(n_dp)
    pair = [
        halving_of(bits[0], first, out_first, rest[:half]),
        halving_of(bits[1], second, out_second, rest[half:]),
    ]
    for one in pair:
        one.begin()
    for unit in interleaved(pair):
        unit()
    for one in pair:
        one.finish()


def grad_sums(first, second, n_dp):
    chunk = first.shape[1:]
    return pl.pallas_call(
        functools.partial(grads_kernel, n_dp),
        out_shape=(
            jax.ShapeDtypeStruct(chunk, jnp.float32),
            jax.ShapeDtypeStruct(chunk, jnp.float32),
        ),
        in_specs=[WHOLE] * 2,
        out_specs=(WHOLE,) * 2,
        scratch_shapes=halving_scratch(n_dp, chunk) + halving_scratch(n_dp, chunk),
        compiler_params=params(3),
        name="sum_grads",
    )(first, second)


def matmul(left, right, left_dim, right_dim):
    return lax.dot_general(
        left, right, (((left_dim,), (right_dim,)), ((), ())), preferred_element_type=jnp.float32
    )


def attend_kernel(spans, queries, keys, values, grads, context, d_queries, d_keys, d_values):
    scaling = DH ** (-0.5)
    wide = keys.shape[0] // spans
    for span in range(spans):
        for head in range(HEADS_AT_ONCE):
            columns = pl.ds(head * DH, DH)
            own = (pl.ds(span * SPAN, SPAN), columns)
            seen = (pl.ds(span * wide, wide), columns)
            q, g, k, v = queries[own], grads[own], keys[seen], values[seen]
            scores = matmul(q, k, 1, 1) * scaling
            weights = jnp.exp(scores - jnp.max(scores, axis=-1, keepdims=True))
            probs_wide = weights / jnp.sum(weights, axis=-1, keepdims=True)
            probs = probs_wide.astype(jnp.bfloat16)
            context[own] = matmul(probs, v, 1, 0).astype(jnp.bfloat16)
            d_probs = matmul(g, v, 1, 1)
            inner = jnp.sum(d_probs * probs_wide, axis=-1, keepdims=True)
            d_scores = (probs_wide * (d_probs - inner) * scaling).astype(jnp.bfloat16)
            d_queries[own] = matmul(d_scores, k, 1, 0).astype(jnp.bfloat16)
            d_keys[seen] = matmul(d_scores, q, 0, 0).astype(jnp.bfloat16)
            d_values[seen] = matmul(probs, g, 0, 0).astype(jnp.bfloat16)


def attend(queries, keys, values, grads, spans):
    rows, columns = queries.shape
    count = keys.shape[0]
    narrow = pl.BlockSpec((rows, DH * HEADS_AT_ONCE), lambda head: (0, head))
    tall = pl.BlockSpec((count, DH * HEADS_AT_ONCE), lambda head: (0, head))
    small = jax.ShapeDtypeStruct((rows, columns), jnp.bfloat16)
    large = jax.ShapeDtypeStruct((count, columns), jnp.bfloat16)
    return pl.pallas_call(
        functools.partial(attend_kernel, spans),
        out_shape=(small, small, large, large),
        grid=(columns // (DH * HEADS_AT_ONCE),),
        in_specs=[narrow, tall, tall, narrow],
        out_specs=(narrow, narrow, tall, tall),
        compiler_params=pltpu.CompilerParams(vmem_limit_bytes=VMEM_BYTES),
        name="attend",
    )(queries, keys, values, grads)


def per_device(queries, neighbours, targets, counts, in_weight, out_weight, kv_weight, d_context):
    length, holding, width = neighbours.shape
    n_dp, n_mp = lax.axis_size("dp"), lax.axis_size("mp")
    spans = queries.shape[0] // SPAN
    blocks = NEIGH * spans
    tokens = blocks * length
    is_live = jnp.arange(holding, dtype=jnp.int32) < counts[0]
    owners = jnp.arange(n_dp, dtype=jnp.int32)
    chosen = jnp.logical_and((targets // blocks)[None, :] == owners[:, None], is_live[None, :])
    tags = jnp.sum(jnp.where(chosen, (targets % blocks)[None, :] + 1, 0), axis=1)
    picks = chosen.astype(jnp.bfloat16)

    def picked(rows):
        return jnp.einsum("oh,thd->otd", picks, rows, preferred_element_type=jnp.float32).astype(
            jnp.bfloat16
        )

    split = max(16, length // (2 * n_mp))
    straight = length - split * n_mp
    own = lax.dynamic_slice_in_dim(
        neighbours, straight + lax.axis_index("mp") * split, split, 0
    )
    tag_rows = jnp.broadcast_to(
        tags.astype(jnp.bfloat16)[:, None, None], (n_dp, TAG_ROWS, width)
    )
    messages = [jnp.concatenate([picked(own), tag_rows], axis=1)]
    if straight:
        messages.append(picked(neighbours[:straight]))
    raw = route(messages, n_dp, n_mp, blocks, length, straight, split).reshape(tokens, width)

    normed = rms_normed(raw)
    hidden_pre = jnp.dot(normed, in_weight, preferred_element_type=jnp.float32)
    activated = gelu_value(hidden_pre).astype(jnp.bfloat16)
    part = jnp.dot(activated, out_weight, preferred_element_type=jnp.float32).astype(jnp.bfloat16)
    sliced = (CHAIN_CHUNKS, tokens // CHAIN_CHUNKS, width)
    encoded = sum_over_mp(part.reshape(sliced), raw.reshape(sliced), n_mp).reshape(tokens, width)

    key_weight, value_weight = kv_weight[:, 0], kv_weight[:, 1]
    keys = jnp.dot(encoded, key_weight, preferred_element_type=jnp.float32).astype(jnp.bfloat16)
    values = jnp.dot(encoded, value_weight, preferred_element_type=jnp.float32).astype(
        jnp.bfloat16
    )
    context, d_queries, d_keys, d_values = attend(queries, keys, values, d_context, spans)

    back = (matmul(d_keys, key_weight, 1, 1) + matmul(d_values, value_weight, 1, 1)).astype(
        jnp.bfloat16
    )
    chunked = (n_dp, width // n_dp, -1)
    key_terms = matmul(encoded, d_keys, 0, 0).astype(jnp.bfloat16).reshape(chunked)
    value_terms = matmul(encoded, d_values, 0, 0).astype(jnp.bfloat16).reshape(chunked)
    d_encoded, grad_key, grad_value = back_sums(
        back.reshape(sliced), key_terms, value_terms, n_mp, n_dp
    )
    d_encoded = d_encoded.reshape(tokens, width)

    d_act = matmul(d_encoded, out_weight, 1, 1)
    d_pre = (d_act * gelu_slope(hidden_pre)).astype(jnp.bfloat16)
    in_terms = matmul(normed, d_pre, 0, 0).astype(jnp.bfloat16).reshape(chunked)
    out_terms = matmul(d_encoded, activated, 0, 0).astype(jnp.bfloat16).reshape(chunked)
    grad_in, grad_out_t = grad_sums(in_terms, out_terms, n_dp)
    return (
        context,
        d_queries,
        jnp.stack([grad_key, grad_value], axis=1),
        grad_in,
        grad_out_t.T,
    )


def solution(mesh):
    placed = (
        P("dp", "mp"),
        P(None, "dp", None),
        P("dp"),
        P("dp"),
        P(None, "mp"),
        P("mp", None),
        P(None, None, "mp"),
        P("dp", "mp"),
    )
    return jax.shard_map(
        per_device,
        mesh=mesh,
        in_specs=placed,
        out_specs=(P("dp", "mp"), P("dp", "mp"), P("dp", None, "mp"), P("dp", "mp"), P("mp", "dp")),
        check_vma=False,
    )
```

```python
import functools

import jax
import jax.numpy as jnp
from jax import lax
from jax.experimental import pallas as pl
from jax.experimental.pallas import tpu as pltpu
from jax.sharding import PartitionSpec as P

DH = 128
SPAN = 64
NEIGH = 2
TAG_ROWS = 16
CHAIN_CHUNKS = 16
CHAIN_LAG = 7
CHAIN_WINDOW = 4
HEADS_AT_ONCE = 4
VMEM_BYTES = 24 * 1024 * 1024


GELU_C = 0.7978845608028654
GELU_A = 0.044715
EPSILON = 1e-06

WHOLE = pl.BlockSpec(memory_space=pltpu.VMEM)


def gelu_value(values):
    inner = GELU_C * (values + GELU_A * values * values * values)
    return 0.5 * values * (1.0 + jnp.tanh(inner))


def gelu_slope(values):
    inner = GELU_C * (values + GELU_A * values * values * values)
    tanh_value = jnp.tanh(inner)
    return 0.5 * (1.0 + tanh_value) + 0.5 * values * (1.0 - tanh_value * tanh_value) * GELU_C * (
        1.0 + 3.0 * GELU_A * values * values
    )


def rms_normed(rows):
    wide = rows.astype(jnp.float32)
    mean_square = jnp.mean(wide * wide, axis=-1, keepdims=True)
    return (wide * lax.rsqrt(mean_square + EPSILON)).astype(jnp.bfloat16)


def ring_peer(axis, step):
    size = lax.axis_size(axis)
    return {axis: lax.rem(lax.axis_index(axis) + step, size)}


def flip_partner(bit):
    me = lax.axis_index("dp")
    mine = lax.rem(lax.div(me, 1 << bit), 2)
    return {"dp": me + (1 - 2 * mine) * (1 << bit)}, mine


def greet(peers):
    barrier = pltpu.get_barrier_semaphore()
    for peer in peers:
        pl.semaphore_signal(barrier, inc=1, device_id=peer, device_id_type=pl.DeviceIdType.MESH)
    pl.semaphore_wait(barrier, len(peers))


def remote(src, dst, send_sem, recv_sem, peer):
    return pltpu.make_async_remote_copy(
        src_ref=src,
        dst_ref=dst,
        send_sem=send_sem,
        recv_sem=recv_sem,
        device_id=peer,
        device_id_type=pl.DeviceIdType.MESH,
    )


class ChainOverMp:
    def __init__(self, size, part, raw, out, scratch):
        self.size, self.part, self.raw, self.out = size, part, raw, out
        self.staged, self.landing, self.up_send, self.up_recv, self.out_send, self.out_recv = scratch
        self.me = lax.axis_index("mp")
        self.chunks = part.shape[0]
        self.is_end = jnp.logical_or(self.me == 0, self.me == size - 1)
        self.steps = self.chunks + CHAIN_LAG

    def root(self, chunk):
        return self.size // 2 - 1 + chunk % 2

    def up(self, chunk, toward, source):
        side = 0 if toward > 0 else 1
        return remote(
            source.at[chunk],
            self.landing.at[side, chunk],
            self.up_send.at[chunk],
            self.up_recv.at[side, chunk],
            {"mp": self.me + toward},
        )

    def outward(self, chunk, toward):
        side = 0 if toward > 0 else 1
        return remote(
            self.out.at[chunk],
            self.out.at[chunk],
            self.out_send.at[side, chunk],
            self.out_recv.at[chunk],
            {"mp": self.me + toward},
        )

    def arrived(self, chunk, toward):
        self.up(chunk, toward, self.staged).wait_recv()
        return self.landing[0 if toward > 0 else 1, chunk].astype(jnp.float32)

    def inner_up(self, chunk):
        root = self.root(chunk)
        own = self.part[chunk].astype(jnp.float32)
        for toward, here in ((1, self.me < root), (-1, self.me > root)):

            @pl.when(here)
            def _(toward=toward):
                total = own + self.arrived(chunk, toward)
                self.staged[chunk] = total.astype(jnp.bfloat16)
                self.up(chunk, toward, self.staged).start()

        @pl.when(self.me == root)
        def _():
            total = own + self.arrived(chunk, 1) + self.arrived(chunk, -1)
            if self.raw is not None:
                total = total + self.raw[chunk].astype(jnp.float32)
            self.out[chunk] = total.astype(jnp.bfloat16)
            self.outward(chunk, 1).start()
            self.outward(chunk, -1).start()

    def inner_down(self, chunk):
        root = self.root(chunk)
        for toward, here in ((-1, self.me < root), (1, self.me > root)):

            @pl.when(here)
            def _(toward=toward):
                self.outward(chunk, toward).wait_recv()
                self.outward(chunk, toward).start()

    def end_up(self, chunk):
        for toward, here in ((1, self.me == 0), (-1, self.me == self.size - 1)):

            @pl.when(here)
            def _(toward=toward):
                if chunk >= CHAIN_WINDOW:
                    self.up(chunk - CHAIN_WINDOW, toward, self.part).wait_send()
                self.up(chunk, toward, self.part).start()

    def step(self, index):
        @pl.when(self.is_end)
        def _():
            if index < self.chunks:
                self.end_up(index)

        @pl.when(jnp.logical_not(self.is_end))
        def _():
            if index < self.chunks:
                self.inner_up(index)
            if index >= CHAIN_LAG:
                self.inner_down(index - CHAIN_LAG)

    def finish(self):
        for toward, here in ((1, self.me == 0), (-1, self.me == self.size - 1)):

            @pl.when(here)
            def _(toward=toward):
                for chunk in range(self.chunks):
                    self.outward(chunk, toward).wait_recv()
                for chunk in range(self.chunks - CHAIN_WINDOW, self.chunks):
                    self.up(chunk, toward, self.part).wait_send()

        @pl.when(jnp.logical_not(self.is_end))
        def _():
            for chunk in range(self.chunks):
                root = self.root(chunk)
                for toward, here in ((1, self.me < root), (-1, self.me > root)):

                    @pl.when(here)
                    def _(toward=toward):
                        self.up(chunk, toward, self.staged).wait_send()
                        self.outward(chunk, -toward).wait_send()

                @pl.when(self.me == root)
                def _():
                    self.outward(chunk, 1).wait_send()
                    self.outward(chunk, -1).wait_send()


class HalvingOverDp:
    def __init__(self, bits, source, out, buffers, sends, recvs):
        self.bits, self.source, self.out, self.buffers = bits, source, out, buffers
        self.sends, self.recvs = sends, recvs
        self.flips = [flip_partner(bit) for bit in bits]
        self.stages = len(bits)

    def held(self, stage, group, low):
        wanted = (low,) + group
        if stage > 0:
            return self.buffers[stage - 1].at[self.slot(wanted)]
        return self.source.at[sum(value * (1 << bit) for value, bit in zip(wanted, self.bits))]

    def slot(self, group):
        return sum((value * (1 << place) for place, value in enumerate(group)), 0)

    def copy(self, stage, group):
        peer, mine = self.flips[stage]
        slot = self.slot(group)
        return remote(
            self.held(stage, group, 1 - mine),
            self.buffers[stage].at[slot],
            self.sends[stage].at[slot],
            self.recvs[stage].at[slot],
            peer,
        )

    def orders(self, stage):
        if stage == self.stages - 1:
            return [()]
        later = self.orders(stage + 1)
        mine = self.flips[stage + 1][1]
        return [(1 - mine,) + group for group in later] + [(mine,) + group for group in later]

    def begin(self):
        for group in self.orders(0):
            self.copy(0, group).start()

    def units(self):
        return [
            functools.partial(self.unit, stage, place)
            for stage in range(self.stages - 1)
            for place in range(len(self.orders(stage)))
        ] + [self.last]

    def unit(self, stage, place):
        mine = self.flips[stage][1]
        orders = self.orders(stage)
        group = orders[place]
        buffer = self.buffers[stage]
        self.copy(stage, group).wait_recv()
        slot = self.slot(group)
        kept = self.held(stage, group, mine)[...].astype(jnp.float32)
        buffer[slot] = (kept + buffer[slot].astype(jnp.float32)).astype(jnp.bfloat16)
        if place < len(orders) // 2:
            self.copy(stage + 1, self.orders(stage + 1)[place]).start()

    def last(self):
        stage = self.stages - 1
        mine = self.flips[stage][1]
        self.copy(stage, ()).wait_recv()
        kept = self.held(stage, (), mine)[...].astype(jnp.float32)
        self.out[...] = kept + self.buffers[stage][0].astype(jnp.float32)

    def finish(self):
        for stage in range(self.stages):
            for group in self.orders(stage):
                self.copy(stage, group).wait_send()


def dp_bits(count):
    total = count.bit_length() - 1
    forward = list(range(total))
    return forward, forward[:1] + forward[:0:-1]


def halving_scratch(count, chunk):
    stages = count.bit_length() - 1
    sizes = [count >> (stage + 1) for stage in range(stages)]
    return (
        [pltpu.VMEM((size,) + chunk, jnp.bfloat16) for size in sizes]
        + [pltpu.SemaphoreType.DMA((size,)) for size in sizes]
        + [pltpu.SemaphoreType.DMA((size,)) for size in sizes]
    )


def halving_of(bits, source, out, scratch):
    stages = len(bits)
    return HalvingOverDp(
        bits, source, out, scratch[:stages], scratch[stages : 2 * stages], scratch[2 * stages :]
    )


def mp_scratch(chunks, rows, width):
    return [
        pltpu.VMEM((chunks, rows, width), jnp.bfloat16),
        pltpu.VMEM((2, chunks, rows, width), jnp.bfloat16),
        pltpu.SemaphoreType.DMA((chunks,)),
        pltpu.SemaphoreType.DMA((2, chunks)),
        pltpu.SemaphoreType.DMA((2, chunks)),
        pltpu.SemaphoreType.DMA((chunks,)),
    ]


def params(collective_id):
    return pltpu.CompilerParams(
        collective_id=collective_id, has_side_effects=True, vmem_limit_bytes=VMEM_BYTES
    )


def mp_peers():
    return [ring_peer("mp", step) for step in range(1, lax.axis_size("mp"))]


def dp_flip_peers(count):
    return [flip_partner(bit)[0] for bit in range(count.bit_length() - 1)]


def route_kernel(n_dp, n_mp, straight, split, pairs, *refs):
    if straight:
        message, whole, out, key_out, value_out, landing, whole_landing, *sems = refs
    else:
        message, out, key_out, value_out, landing, *sems = refs
    greet([ring_peer("dp", step) for step in range(1, n_dp)] + mp_peers())
    blocks = out.shape[0]
    me_dp, me_mp = lax.axis_index("dp"), lax.axis_index("mp")

    def exchange(source, target, step, send, recv):
        peer = ring_peer("dp", step)
        return remote(
            source.at[peer["dp"]], target.at[step - 1], send.at[step - 1], recv.at[step - 1], peer
        )

    def parts(step):
        return exchange(message, landing, step, sems[0], sems[1])

    def wholes(step):
        return exchange(whole, whole_landing, step, sems[4], sems[5])

    others = range(1, n_dp)
    for step in others:
        parts(step).start()
    if straight:
        for step in others:
            wholes(step).start()

    @pl.loop(0, pairs.shape[0] // 16)
    def _(index):
        rows = pl.ds(pl.multiple_of(index * 16, 16), 16)
        key_out[rows, :] = pairs[rows, 0, :]
        value_out[rows, :] = pairs[rows, 1, :]

    def tags_of(rows):
        return rows.astype(jnp.float32)[:1]

    for step in others:
        parts(step).wait_recv()
    data_rows = pl.ds(0, split)
    tag_rows = pl.ds(split, TAG_ROWS)
    tags = [tags_of(message[me_dp, tag_rows])] + [
        tags_of(landing[step - 1, tag_rows]) for step in others
    ]

    def place(own, arrived, first, where):
        sources = [own[me_dp, first]] + [arrived[step - 1, first] for step in others]
        sources = [rows.astype(jnp.float32) for rows in sources]
        for block in range(blocks):
            value = jnp.zeros_like(sources[0])
            for tag, rows in zip(tags, sources):
                value = jnp.where(tag == block + 1.0, rows, value)
            out[block, where] = value.astype(jnp.bfloat16)

    mine = pl.ds(pl.multiple_of(straight + me_mp * split, 16), split)
    place(message, landing, data_rows, mine)

    def gather(step):
        return remote(
            out.at[:, mine],
            out.at[:, mine],
            sems[2].at[step - 1],
            sems[3].at[step - 1],
            ring_peer("mp", step),
        )

    for step in range(1, n_mp):
        gather(step).start()
    if straight:
        for step in others:
            wholes(step).wait_recv()
        for first in range(0, straight, 16):
            rows = pl.ds(first, 16)
            place(whole, whole_landing, rows, rows)
    for step in range(1, n_mp):
        gather(step).wait_recv()
    for step in others:
        parts(step).wait_send()
        if straight:
            wholes(step).wait_send()
    for step in range(1, n_mp):
        gather(step).wait_send()


def route(pairs, messages, n_dp, n_mp, blocks, length, straight, split):
    width = messages[0].shape[2]
    half = jax.ShapeDtypeStruct((pairs.shape[0], pairs.shape[2]), jnp.bfloat16)
    return pl.pallas_call(
        functools.partial(route_kernel, n_dp, n_mp, straight, split),
        out_shape=(jax.ShapeDtypeStruct((blocks, length, width), jnp.bfloat16), half, half),
        in_specs=[WHOLE] * (1 + len(messages)),
        out_specs=(WHOLE,) * 3,
        scratch_shapes=[
            pltpu.VMEM((n_dp - 1,) + message.shape[1:], jnp.bfloat16) for message in messages
        ]
        + [
            pltpu.SemaphoreType.DMA((n_dp - 1,)),
            pltpu.SemaphoreType.DMA((n_dp - 1,)),
            pltpu.SemaphoreType.DMA((n_mp - 1,)),
            pltpu.SemaphoreType.DMA((n_mp - 1,)),
            pltpu.SemaphoreType.DMA((n_dp - 1,)),
            pltpu.SemaphoreType.DMA((n_dp - 1,)),
        ],
        compiler_params=params(0),
        name="route",
    )(pairs, *messages)


def sum_kernel(n_mp, part, raw, out, *scratch):
    greet(mp_peers())
    total = ChainOverMp(n_mp, part, raw, out, scratch)
    for index in range(total.steps):
        total.step(index)
    total.finish()


def sum_over_mp(part, raw, n_mp):
    rows, width = part.shape[1:]
    return pl.pallas_call(
        functools.partial(sum_kernel, n_mp),
        out_shape=jax.ShapeDtypeStruct(part.shape, jnp.bfloat16),
        in_specs=[WHOLE, WHOLE],
        out_specs=WHOLE,
        scratch_shapes=mp_scratch(part.shape[0], rows, width),
        compiler_params=params(1),
        name="sum_encoded",
    )(part, raw)


def interleaved(pair):
    return [unit for both in zip(*(one.units() for one in pair)) for unit in both]


def back_kernel(n_mp, n_dp, part, first, second, out, out_first, out_second, *rest):
    greet(mp_peers() + dp_flip_peers(n_dp))
    chain, rest = rest[:6], rest[6:]
    half = len(rest) // 2
    bits = dp_bits(n_dp)
    total = ChainOverMp(n_mp, part, None, out, chain)
    pair = [
        halving_of(bits[0], first, out_first, rest[:half]),
        halving_of(bits[1], second, out_second, rest[half:]),
    ]
    for one in pair:
        one.begin()
    units = interleaved(pair)
    for index in range(total.steps):
        total.step(index)
        if index > 0 and units:
            units.pop(0)()
    for unit in units:
        unit()
    total.finish()
    for one in pair:
        one.finish()


def back_sums(part, first, second, n_mp, n_dp):
    rows, width = part.shape[1:]
    chunk = first.shape[1:]
    return pl.pallas_call(
        functools.partial(back_kernel, n_mp, n_dp),
        out_shape=(
            jax.ShapeDtypeStruct(part.shape, jnp.bfloat16),
            jax.ShapeDtypeStruct(chunk, jnp.float32),
            jax.ShapeDtypeStruct(chunk, jnp.float32),
        ),
        in_specs=[WHOLE] * 3,
        out_specs=(WHOLE,) * 3,
        scratch_shapes=mp_scratch(part.shape[0], rows, width)
        + halving_scratch(n_dp, chunk)
        + halving_scratch(n_dp, chunk),
        compiler_params=params(2),
        name="sum_back",
    )(part, first, second)


def grads_kernel(n_dp, first, second, out_first, out_second, *rest):
    greet(dp_flip_peers(n_dp))
    half = len(rest) // 2
    bits = dp_bits(n_dp)
    pair = [
        halving_of(bits[0], first, out_first, rest[:half]),
        halving_of(bits[1], second, out_second, rest[half:]),
    ]
    for one in pair:
        one.begin()
    for unit in interleaved(pair):
        unit()
    for one in pair:
        one.finish()


def grad_sums(first, second, n_dp):
    chunk = first.shape[1:]
    return pl.pallas_call(
        functools.partial(grads_kernel, n_dp),
        out_shape=(
            jax.ShapeDtypeStruct(chunk, jnp.float32),
            jax.ShapeDtypeStruct(chunk, jnp.float32),
        ),
        in_specs=[WHOLE] * 2,
        out_specs=(WHOLE,) * 2,
        scratch_shapes=halving_scratch(n_dp, chunk) + halving_scratch(n_dp, chunk),
        compiler_params=params(3),
        name="sum_grads",
    )(first, second)


def matmul(left, right, left_dim, right_dim):
    return lax.dot_general(
        left, right, (((left_dim,), (right_dim,)), ((), ())), preferred_element_type=jnp.float32
    )


def attend_kernel(spans, queries, keys, values, grads, context, d_queries, d_keys, d_values):
    scaling = DH ** (-0.5)
    wide = keys.shape[0] // spans
    units = []
    for span in range(spans):
        for head in range(HEADS_AT_ONCE):
            columns = pl.ds(head * DH, DH)
            units.append(
                ((pl.ds(span * SPAN, SPAN), columns), (pl.ds(span * wide, wide), columns))
            )
    scores = [matmul(queries[own], keys[seen], 1, 1) * scaling for own, seen in units]
    d_probs = [matmul(grads[own], values[seen], 1, 1) for own, seen in units]
    weights = [jnp.exp(one - jnp.max(one, axis=-1, keepdims=True)) for one in scores]
    wides = [one / jnp.sum(one, axis=-1, keepdims=True) for one in weights]
    probs = [one.astype(jnp.bfloat16) for one in wides]
    inners = [jnp.sum(d * p, axis=-1, keepdims=True) for d, p in zip(d_probs, wides)]
    d_scores = [
        (p * (d - inner) * scaling).astype(jnp.bfloat16)
        for p, d, inner in zip(wides, d_probs, inners)
    ]
    for (own, seen), p in zip(units, probs):
        context[own] = matmul(p, values[seen], 1, 0).astype(jnp.bfloat16)
    for (own, seen), d in zip(units, d_scores):
        d_queries[own] = matmul(d, keys[seen], 1, 0).astype(jnp.bfloat16)
    for (own, seen), p in zip(units, probs):
        d_values[seen] = matmul(p, grads[own], 0, 0).astype(jnp.bfloat16)
    for (own, seen), d in zip(units, d_scores):
        d_keys[seen] = matmul(d, queries[own], 0, 0).astype(jnp.bfloat16)


def attend(queries, keys, values, grads, spans):
    rows, columns = queries.shape
    count = keys.shape[0]
    narrow = pl.BlockSpec((rows, DH * HEADS_AT_ONCE), lambda head: (0, head))
    tall = pl.BlockSpec((count, DH * HEADS_AT_ONCE), lambda head: (0, head))
    small = jax.ShapeDtypeStruct((rows, columns), jnp.bfloat16)
    large = jax.ShapeDtypeStruct((count, columns), jnp.bfloat16)
    return pl.pallas_call(
        functools.partial(attend_kernel, spans),
        out_shape=(small, small, large, large),
        grid=(columns // (DH * HEADS_AT_ONCE),),
        in_specs=[narrow, tall, tall, narrow],
        out_specs=(narrow, narrow, tall, tall),
        compiler_params=pltpu.CompilerParams(vmem_limit_bytes=VMEM_BYTES),
        name="attend",
    )(queries, keys, values, grads)


def per_device(queries, neighbours, targets, counts, in_weight, out_weight, kv_weight, d_context):
    length, holding, width = neighbours.shape
    n_dp, n_mp = lax.axis_size("dp"), lax.axis_size("mp")
    spans = queries.shape[0] // SPAN
    blocks = NEIGH * spans
    tokens = blocks * length
    is_live = jnp.arange(holding, dtype=jnp.int32) < counts[0]
    owners = jnp.arange(n_dp, dtype=jnp.int32)
    chosen = jnp.logical_and((targets // blocks)[None, :] == owners[:, None], is_live[None, :])
    tags = jnp.sum(jnp.where(chosen, (targets % blocks)[None, :] + 1, 0), axis=1)
    picks = chosen.astype(jnp.bfloat16)

    def picked(rows):
        return jnp.einsum("oh,thd->otd", picks, rows, preferred_element_type=jnp.float32).astype(
            jnp.bfloat16
        )

    split = max(16, length // (2 * n_mp))
    straight = length - split * n_mp
    own = lax.dynamic_slice_in_dim(
        neighbours, straight + lax.axis_index("mp") * split, split, 0
    )
    tag_rows = jnp.broadcast_to(
        tags.astype(jnp.bfloat16)[:, None, None], (n_dp, TAG_ROWS, width)
    )
    messages = [jnp.concatenate([picked(own), tag_rows], axis=1)]
    if straight:
        messages.append(picked(neighbours[:straight]))
    raw, key_weight, value_weight = route(
        kv_weight, messages, n_dp, n_mp, blocks, length, straight, split
    )
    raw = raw.reshape(tokens, width)

    normed = rms_normed(raw)
    hidden_pre = jnp.dot(normed, in_weight, preferred_element_type=jnp.float32)
    activated = gelu_value(hidden_pre).astype(jnp.bfloat16)
    part = jnp.dot(activated, out_weight, preferred_element_type=jnp.float32).astype(jnp.bfloat16)
    sliced = (CHAIN_CHUNKS, tokens // CHAIN_CHUNKS, width)
    encoded = sum_over_mp(part.reshape(sliced), raw.reshape(sliced), n_mp).reshape(tokens, width)

    keys = jnp.dot(encoded, key_weight, preferred_element_type=jnp.float32).astype(jnp.bfloat16)
    values = jnp.dot(encoded, value_weight, preferred_element_type=jnp.float32).astype(
        jnp.bfloat16
    )
    context, d_queries, d_keys, d_values = attend(queries, keys, values, d_context, spans)

    back = (matmul(d_keys, key_weight, 1, 1) + matmul(d_values, value_weight, 1, 1)).astype(
        jnp.bfloat16
    )
    chunked = (n_dp, width // n_dp, -1)
    key_terms = matmul(encoded, d_keys, 0, 0).astype(jnp.bfloat16).reshape(chunked)
    value_terms = matmul(encoded, d_values, 0, 0).astype(jnp.bfloat16).reshape(chunked)
    d_encoded, grad_key, grad_value = back_sums(
        back.reshape(sliced), key_terms, value_terms, n_mp, n_dp
    )
    d_encoded = d_encoded.reshape(tokens, width)

    d_act = matmul(d_encoded, out_weight, 1, 1)
    d_pre = (d_act * gelu_slope(hidden_pre)).astype(jnp.bfloat16)
    in_terms = matmul(normed, d_pre, 0, 0).astype(jnp.bfloat16).reshape(chunked)
    out_terms = matmul(d_encoded, activated, 0, 0).astype(jnp.bfloat16).reshape(chunked)
    grad_in, grad_out_t = grad_sums(in_terms, out_terms, n_dp)
    return (
        context,
        d_queries,
        jnp.stack([grad_key, grad_value], axis=1),
        grad_in,
        grad_out_t.T,
    )


def solution(mesh):
    placed = (
        P("dp", "mp"),
        P(None, "dp", None),
        P("dp"),
        P("dp"),
        P(None, "mp"),
        P("mp", None),
        P(None, None, "mp"),
        P("dp", "mp"),
    )
    return jax.shard_map(
        per_device,
        mesh=mesh,
        in_specs=placed,
        out_specs=(P("dp", "mp"), P("dp", "mp"), P("dp", None, "mp"), P("dp", "mp"), P("mp", "dp")),
        check_vma=False,
    )
```

```python
import functools

import jax
import jax.numpy as jnp
from jax import lax
from jax.experimental import pallas as pl
from jax.experimental.pallas import tpu as pltpu
from jax.sharding import PartitionSpec as P

DH = 128
SPAN = 64
NEIGH = 2
TAG_ROWS = 16
CHAIN_CHUNKS = 16
ROOT_LAG = 4
CHAIN_LAG = 8
CHAIN_WINDOW = 4
HEADS_AT_ONCE = 4
VMEM_BYTES = 24 * 1024 * 1024


GELU_C = 0.7978845608028654
GELU_A = 0.044715
EPSILON = 1e-06

WHOLE = pl.BlockSpec(memory_space=pltpu.VMEM)


def gelu_value(values):
    inner = GELU_C * (values + GELU_A * values * values * values)
    return 0.5 * values * (1.0 + jnp.tanh(inner))


def gelu_slope(values):
    inner = GELU_C * (values + GELU_A * values * values * values)
    tanh_value = jnp.tanh(inner)
    return 0.5 * (1.0 + tanh_value) + 0.5 * values * (1.0 - tanh_value * tanh_value) * GELU_C * (
        1.0 + 3.0 * GELU_A * values * values
    )


def rms_normed(rows):
    wide = rows.astype(jnp.float32)
    mean_square = jnp.mean(wide * wide, axis=-1, keepdims=True)
    return (wide * lax.rsqrt(mean_square + EPSILON)).astype(jnp.bfloat16)


def ring_peer(axis, step):
    size = lax.axis_size(axis)
    return {axis: lax.rem(lax.axis_index(axis) + step, size)}


def flip_partner(bit):
    me = lax.axis_index("dp")
    mine = lax.rem(lax.div(me, 1 << bit), 2)
    return {"dp": me + (1 - 2 * mine) * (1 << bit)}, mine


def greet(peers):
    barrier = pltpu.get_barrier_semaphore()
    for peer in peers:
        pl.semaphore_signal(barrier, inc=1, device_id=peer, device_id_type=pl.DeviceIdType.MESH)
    pl.semaphore_wait(barrier, len(peers))


def remote(src, dst, send_sem, recv_sem, peer):
    return pltpu.make_async_remote_copy(
        src_ref=src,
        dst_ref=dst,
        send_sem=send_sem,
        recv_sem=recv_sem,
        device_id=peer,
        device_id_type=pl.DeviceIdType.MESH,
    )


class ChainOverMp:
    def __init__(self, size, part, raw, out, scratch):
        self.size, self.part, self.raw, self.out = size, part, raw, out
        self.staged, self.landing, self.up_send, self.up_recv, self.out_send, self.out_recv = scratch
        self.me = lax.axis_index("mp")
        self.chunks = part.shape[0]
        self.is_end = jnp.logical_or(self.me == 0, self.me == size - 1)
        self.steps = self.chunks + CHAIN_LAG

    def root(self, chunk):
        return self.size // 2 - 1 + chunk % 2

    def up(self, chunk, toward, source):
        side = 0 if toward > 0 else 1
        return remote(
            source.at[chunk],
            self.landing.at[side, chunk],
            self.up_send.at[chunk],
            self.up_recv.at[side, chunk],
            {"mp": self.me + toward},
        )

    def outward(self, chunk, toward):
        side = 0 if toward > 0 else 1
        return remote(
            self.out.at[chunk],
            self.out.at[chunk],
            self.out_send.at[side, chunk],
            self.out_recv.at[chunk],
            {"mp": self.me + toward},
        )

    def arrived(self, chunk, toward):
        self.up(chunk, toward, self.staged).wait_recv()
        return self.landing[0 if toward > 0 else 1, chunk].astype(jnp.float32)

    def inner_up(self, chunk):
        root = self.root(chunk)
        for toward, here in ((1, self.me < root), (-1, self.me > root)):

            @pl.when(here)
            def _(toward=toward):
                total = self.part[chunk].astype(jnp.float32) + self.arrived(chunk, toward)
                self.staged[chunk] = total.astype(jnp.bfloat16)
                self.up(chunk, toward, self.staged).start()

    def inner_root(self, chunk):
        @pl.when(self.me == self.root(chunk))
        def _():
            total = self.part[chunk].astype(jnp.float32)
            total = total + self.arrived(chunk, 1) + self.arrived(chunk, -1)
            if self.raw is not None:
                total = total + self.raw[chunk].astype(jnp.float32)
            self.out[chunk] = total.astype(jnp.bfloat16)
            self.outward(chunk, 1).start()
            self.outward(chunk, -1).start()

    def inner_down(self, chunk):
        root = self.root(chunk)
        for toward, here in ((-1, self.me < root), (1, self.me > root)):

            @pl.when(here)
            def _(toward=toward):
                self.outward(chunk, toward).wait_recv()
                self.outward(chunk, toward).start()

    def end_up(self, chunk):
        for toward, here in ((1, self.me == 0), (-1, self.me == self.size - 1)):

            @pl.when(here)
            def _(toward=toward):
                if chunk >= CHAIN_WINDOW:
                    self.up(chunk - CHAIN_WINDOW, toward, self.part).wait_send()
                self.up(chunk, toward, self.part).start()

    def step(self, index):
        @pl.when(self.is_end)
        def _():
            if index < self.chunks:
                self.end_up(index)

        @pl.when(jnp.logical_not(self.is_end))
        def _():
            if index < self.chunks:
                self.inner_up(index)
            if 0 <= index - ROOT_LAG < self.chunks:
                self.inner_root(index - ROOT_LAG)
            if index >= CHAIN_LAG:
                self.inner_down(index - CHAIN_LAG)

    def finish(self):
        for toward, here in ((1, self.me == 0), (-1, self.me == self.size - 1)):

            @pl.when(here)
            def _(toward=toward):
                for chunk in range(self.chunks):
                    self.outward(chunk, toward).wait_recv()
                for chunk in range(self.chunks - CHAIN_WINDOW, self.chunks):
                    self.up(chunk, toward, self.part).wait_send()

        @pl.when(jnp.logical_not(self.is_end))
        def _():
            for chunk in range(self.chunks):
                root = self.root(chunk)
                for toward, here in ((1, self.me < root), (-1, self.me > root)):

                    @pl.when(here)
                    def _(toward=toward):
                        self.up(chunk, toward, self.staged).wait_send()
                        self.outward(chunk, -toward).wait_send()

                @pl.when(self.me == root)
                def _():
                    self.outward(chunk, 1).wait_send()
                    self.outward(chunk, -1).wait_send()


class HalvingOverDp:
    def __init__(self, bits, source, out, buffers, sends, recvs):
        self.bits, self.source, self.out, self.buffers = bits, source, out, buffers
        self.sends, self.recvs = sends, recvs
        self.flips = [flip_partner(bit) for bit in bits]
        self.stages = len(bits)

    def held(self, stage, group, low):
        wanted = (low,) + group
        if stage > 0:
            return self.buffers[stage - 1].at[self.slot(wanted)]
        return self.source.at[sum(value * (1 << bit) for value, bit in zip(wanted, self.bits))]

    def slot(self, group):
        return sum((value * (1 << place) for place, value in enumerate(group)), 0)

    def copy(self, stage, group):
        peer, mine = self.flips[stage]
        slot = self.slot(group)
        return remote(
            self.held(stage, group, 1 - mine),
            self.buffers[stage].at[slot],
            self.sends[stage].at[slot],
            self.recvs[stage].at[slot],
            peer,
        )

    def orders(self, stage):
        if stage == self.stages - 1:
            return [()]
        later = self.orders(stage + 1)
        mine = self.flips[stage + 1][1]
        return [(1 - mine,) + group for group in later] + [(mine,) + group for group in later]

    def begin(self):
        for group in self.orders(0):
            self.copy(0, group).start()

    def units(self):
        return [
            functools.partial(self.unit, stage, place)
            for stage in range(self.stages - 1)
            for place in range(len(self.orders(stage)))
        ] + [self.last]

    def unit(self, stage, place):
        mine = self.flips[stage][1]
        orders = self.orders(stage)
        group = orders[place]
        buffer = self.buffers[stage]
        self.copy(stage, group).wait_recv()
        slot = self.slot(group)
        kept = self.held(stage, group, mine)[...].astype(jnp.float32)
        buffer[slot] = (kept + buffer[slot].astype(jnp.float32)).astype(jnp.bfloat16)
        if place < len(orders) // 2:
            self.copy(stage + 1, self.orders(stage + 1)[place]).start()

    def last(self):
        stage = self.stages - 1
        mine = self.flips[stage][1]
        self.copy(stage, ()).wait_recv()
        kept = self.held(stage, (), mine)[...].astype(jnp.float32)
        self.out[...] = kept + self.buffers[stage][0].astype(jnp.float32)

    def finish(self):
        for stage in range(self.stages):
            for group in self.orders(stage):
                self.copy(stage, group).wait_send()


def dp_bits(count):
    total = count.bit_length() - 1
    forward = list(range(total))
    return forward, forward[:1] + forward[:0:-1]


def halving_scratch(count, chunk):
    stages = count.bit_length() - 1
    sizes = [count >> (stage + 1) for stage in range(stages)]
    return (
        [pltpu.VMEM((size,) + chunk, jnp.bfloat16) for size in sizes]
        + [pltpu.SemaphoreType.DMA((size,)) for size in sizes]
        + [pltpu.SemaphoreType.DMA((size,)) for size in sizes]
    )


def halving_of(bits, source, out, scratch):
    stages = len(bits)
    return HalvingOverDp(
        bits, source, out, scratch[:stages], scratch[stages : 2 * stages], scratch[2 * stages :]
    )


def mp_scratch(chunks, rows, width):
    return [
        pltpu.VMEM((chunks, rows, width), jnp.bfloat16),
        pltpu.VMEM((2, chunks, rows, width), jnp.bfloat16),
        pltpu.SemaphoreType.DMA((chunks,)),
        pltpu.SemaphoreType.DMA((2, chunks)),
        pltpu.SemaphoreType.DMA((2, chunks)),
        pltpu.SemaphoreType.DMA((chunks,)),
    ]


def params(collective_id):
    return pltpu.CompilerParams(
        collective_id=collective_id, has_side_effects=True, vmem_limit_bytes=VMEM_BYTES
    )


def mp_peers():
    return [ring_peer("mp", step) for step in range(1, lax.axis_size("mp"))]


def dp_flip_peers(count):
    return [flip_partner(bit)[0] for bit in range(count.bit_length() - 1)]


def route_kernel(n_dp, n_mp, straight, split, pairs, *refs):
    if straight:
        message, whole, out, key_out, value_out, landing, whole_landing, *sems = refs
    else:
        message, out, key_out, value_out, landing, *sems = refs
    *sems, pairs_here, pairs_sem = sems
    fetch = pltpu.make_async_copy(pairs, pairs_here, pairs_sem)
    fetch.start()
    greet([ring_peer("dp", step) for step in range(1, n_dp)] + mp_peers())
    blocks = out.shape[0]
    me_dp, me_mp = lax.axis_index("dp"), lax.axis_index("mp")

    def exchange(source, target, step, send, recv):
        peer = ring_peer("dp", step)
        return remote(
            source.at[peer["dp"]], target.at[step - 1], send.at[step - 1], recv.at[step - 1], peer
        )

    def parts(step):
        return exchange(message, landing, step, sems[0], sems[1])

    def wholes(step):
        return exchange(whole, whole_landing, step, sems[4], sems[5])

    others = range(1, n_dp)
    for step in others:
        parts(step).start()
    if straight:
        for step in others:
            wholes(step).start()

    fetch.wait()

    @pl.loop(0, pairs.shape[0] // 16)
    def _(index):
        rows = pl.ds(pl.multiple_of(index * 16, 16), 16)
        key_out[rows, :] = pairs_here[rows, 0, :]
        value_out[rows, :] = pairs_here[rows, 1, :]

    def tags_of(rows):
        return rows.astype(jnp.float32)[:1]

    for step in others:
        parts(step).wait_recv()
    data_rows = pl.ds(0, split)
    tag_rows = pl.ds(split, TAG_ROWS)
    tags = [tags_of(message[me_dp, tag_rows])] + [
        tags_of(landing[step - 1, tag_rows]) for step in others
    ]

    def place(own, arrived, first, where):
        sources = [own[me_dp, first]] + [arrived[step - 1, first] for step in others]
        sources = [rows.astype(jnp.float32) for rows in sources]
        for block in range(blocks):
            value = jnp.zeros_like(sources[0])
            for tag, rows in zip(tags, sources):
                value = jnp.where(tag == block + 1.0, rows, value)
            out[block, where] = value.astype(jnp.bfloat16)

    mine = pl.ds(pl.multiple_of(straight + me_mp * split, 16), split)
    place(message, landing, data_rows, mine)

    def gather(step):
        return remote(
            out.at[:, mine],
            out.at[:, mine],
            sems[2].at[step - 1],
            sems[3].at[step - 1],
            ring_peer("mp", step),
        )

    for step in range(1, n_mp):
        gather(step).start()
    if straight:
        for step in others:
            wholes(step).wait_recv()
        for first in range(0, straight, 16):
            rows = pl.ds(first, 16)
            place(whole, whole_landing, rows, rows)
    for step in range(1, n_mp):
        gather(step).wait_recv()
    for step in others:
        parts(step).wait_send()
        if straight:
            wholes(step).wait_send()
    for step in range(1, n_mp):
        gather(step).wait_send()


def route(pairs, messages, n_dp, n_mp, blocks, length, straight, split):
    width = messages[0].shape[2]
    half = jax.ShapeDtypeStruct((pairs.shape[0], pairs.shape[2]), jnp.bfloat16)
    return pl.pallas_call(
        functools.partial(route_kernel, n_dp, n_mp, straight, split),
        out_shape=(jax.ShapeDtypeStruct((blocks, length, width), jnp.bfloat16), half, half),
        in_specs=[pl.BlockSpec(memory_space=pltpu.HBM)] + [WHOLE] * len(messages),
        out_specs=(WHOLE,) * 3,
        scratch_shapes=[
            pltpu.VMEM((n_dp - 1,) + message.shape[1:], jnp.bfloat16) for message in messages
        ]
        + [
            pltpu.SemaphoreType.DMA((n_dp - 1,)),
            pltpu.SemaphoreType.DMA((n_dp - 1,)),
            pltpu.SemaphoreType.DMA((n_mp - 1,)),
            pltpu.SemaphoreType.DMA((n_mp - 1,)),
            pltpu.SemaphoreType.DMA((n_dp - 1,)),
            pltpu.SemaphoreType.DMA((n_dp - 1,)),
            pltpu.VMEM(pairs.shape, jnp.bfloat16),
            pltpu.SemaphoreType.DMA,
        ],
        compiler_params=params(0),
        name="route",
    )(pairs, *messages)


def sum_kernel(n_mp, part, raw, out, *scratch):
    greet(mp_peers())
    total = ChainOverMp(n_mp, part, raw, out, scratch)
    for index in range(total.steps):
        total.step(index)
    total.finish()


def sum_over_mp(part, raw, n_mp):
    rows, width = part.shape[1:]
    return pl.pallas_call(
        functools.partial(sum_kernel, n_mp),
        out_shape=jax.ShapeDtypeStruct(part.shape, jnp.bfloat16),
        in_specs=[WHOLE, WHOLE],
        out_specs=WHOLE,
        scratch_shapes=mp_scratch(part.shape[0], rows, width),
        compiler_params=params(1),
        name="sum_encoded",
    )(part, raw)


def interleaved(pair):
    return [unit for both in zip(*(one.units() for one in pair)) for unit in both]


def back_kernel(n_mp, n_dp, part, first, second, out, out_first, out_second, *rest):
    greet(mp_peers() + dp_flip_peers(n_dp))
    chain, rest = rest[:6], rest[6:]
    half = len(rest) // 2
    bits = dp_bits(n_dp)
    total = ChainOverMp(n_mp, part, None, out, chain)
    pair = [
        halving_of(bits[0], first, out_first, rest[:half]),
        halving_of(bits[1], second, out_second, rest[half:]),
    ]
    for one in pair:
        one.begin()
    units = interleaved(pair)
    for index in range(total.steps):
        total.step(index)
        if index > 1 and units:
            units.pop(0)()
    for unit in units:
        unit()
    total.finish()
    for one in pair:
        one.finish()


def back_sums(part, first, second, n_mp, n_dp):
    rows, width = part.shape[1:]
    chunk = first.shape[1:]
    return pl.pallas_call(
        functools.partial(back_kernel, n_mp, n_dp),
        out_shape=(
            jax.ShapeDtypeStruct(part.shape, jnp.bfloat16),
            jax.ShapeDtypeStruct(chunk, jnp.float32),
            jax.ShapeDtypeStruct(chunk, jnp.float32),
        ),
        in_specs=[WHOLE] * 3,
        out_specs=(WHOLE,) * 3,
        scratch_shapes=mp_scratch(part.shape[0], rows, width)
        + halving_scratch(n_dp, chunk)
        + halving_scratch(n_dp, chunk),
        compiler_params=params(2),
        name="sum_back",
    )(part, first, second)


def grads_kernel(n_dp, first, second, out_first, out_second, *rest):
    greet(dp_flip_peers(n_dp))
    half = len(rest) // 2
    bits = dp_bits(n_dp)
    pair = [
        halving_of(bits[0], first, out_first, rest[:half]),
        halving_of(bits[1], second, out_second, rest[half:]),
    ]
    for one in pair:
        one.begin()
    for unit in interleaved(pair):
        unit()
    for one in pair:
        one.finish()


def grad_sums(first, second, n_dp):
    chunk = first.shape[1:]
    return pl.pallas_call(
        functools.partial(grads_kernel, n_dp),
        out_shape=(
            jax.ShapeDtypeStruct(chunk, jnp.float32),
            jax.ShapeDtypeStruct(chunk, jnp.float32),
        ),
        in_specs=[WHOLE] * 2,
        out_specs=(WHOLE,) * 2,
        scratch_shapes=halving_scratch(n_dp, chunk) + halving_scratch(n_dp, chunk),
        compiler_params=params(3),
        name="sum_grads",
    )(first, second)


def matmul(left, right, left_dim, right_dim):
    return lax.dot_general(
        left, right, (((left_dim,), (right_dim,)), ((), ())), preferred_element_type=jnp.float32
    )


def attend_kernel(spans, queries, keys, values, grads, context, d_queries, d_keys, d_values):
    scaling = DH ** (-0.5)
    wide = keys.shape[0] // spans
    units = []
    for span in range(spans):
        for head in range(HEADS_AT_ONCE):
            columns = pl.ds(head * DH, DH)
            units.append(
                ((pl.ds(span * SPAN, SPAN), columns), (pl.ds(span * wide, wide), columns))
            )
    scores = [matmul(queries[own], keys[seen], 1, 1) * scaling for own, seen in units]
    d_probs = [matmul(grads[own], values[seen], 1, 1) for own, seen in units]
    weights = [jnp.exp(one - jnp.max(one, axis=-1, keepdims=True)) for one in scores]
    wides = [one / jnp.sum(one, axis=-1, keepdims=True) for one in weights]
    probs = [one.astype(jnp.bfloat16) for one in wides]
    inners = [jnp.sum(d * p, axis=-1, keepdims=True) for d, p in zip(d_probs, wides)]
    d_scores = [
        (p * (d - inner) * scaling).astype(jnp.bfloat16)
        for p, d, inner in zip(wides, d_probs, inners)
    ]
    for (own, seen), p in zip(units, probs):
        context[own] = matmul(p, values[seen], 1, 0).astype(jnp.bfloat16)
    for (own, seen), d in zip(units, d_scores):
        d_queries[own] = matmul(d, keys[seen], 1, 0).astype(jnp.bfloat16)
    for (own, seen), p in zip(units, probs):
        d_values[seen] = matmul(p, grads[own], 0, 0).astype(jnp.bfloat16)
    for (own, seen), d in zip(units, d_scores):
        d_keys[seen] = matmul(d, queries[own], 0, 0).astype(jnp.bfloat16)


def attend(queries, keys, values, grads, spans):
    rows, columns = queries.shape
    count = keys.shape[0]
    narrow = pl.BlockSpec((rows, DH * HEADS_AT_ONCE), lambda head: (0, head))
    tall = pl.BlockSpec((count, DH * HEADS_AT_ONCE), lambda head: (0, head))
    small = jax.ShapeDtypeStruct((rows, columns), jnp.bfloat16)
    large = jax.ShapeDtypeStruct((count, columns), jnp.bfloat16)
    return pl.pallas_call(
        functools.partial(attend_kernel, spans),
        out_shape=(small, small, large, large),
        grid=(columns // (DH * HEADS_AT_ONCE),),
        in_specs=[narrow, tall, tall, narrow],
        out_specs=(narrow, narrow, tall, tall),
        compiler_params=pltpu.CompilerParams(vmem_limit_bytes=VMEM_BYTES),
        name="attend",
    )(queries, keys, values, grads)


def per_device(queries, neighbours, targets, counts, in_weight, out_weight, kv_weight, d_context):
    length, holding, width = neighbours.shape
    n_dp, n_mp = lax.axis_size("dp"), lax.axis_size("mp")
    spans = queries.shape[0] // SPAN
    blocks = NEIGH * spans
    tokens = blocks * length
    is_live = jnp.arange(holding, dtype=jnp.int32) < counts[0]
    owners = jnp.arange(n_dp, dtype=jnp.int32)
    chosen = jnp.logical_and((targets // blocks)[None, :] == owners[:, None], is_live[None, :])
    tags = jnp.sum(jnp.where(chosen, (targets % blocks)[None, :] + 1, 0), axis=1)
    picks = chosen.astype(jnp.bfloat16)

    def picked(rows):
        return jnp.einsum("oh,thd->otd", picks, rows, preferred_element_type=jnp.float32).astype(
            jnp.bfloat16
        )

    split = max(16, length // (2 * n_mp))
    straight = length - split * n_mp
    own = lax.dynamic_slice_in_dim(
        neighbours, straight + lax.axis_index("mp") * split, split, 0
    )
    tag_rows = jnp.broadcast_to(
        tags.astype(jnp.bfloat16)[:, None, None], (n_dp, TAG_ROWS, width)
    )
    messages = [jnp.concatenate([picked(own), tag_rows], axis=1)]
    if straight:
        messages.append(picked(neighbours[:straight]))
    raw, key_weight, value_weight = route(
        kv_weight, messages, n_dp, n_mp, blocks, length, straight, split
    )
    raw = raw.reshape(tokens, width)

    normed = rms_normed(raw)
    hidden_pre = jnp.dot(normed, in_weight, preferred_element_type=jnp.float32)
    activated = gelu_value(hidden_pre).astype(jnp.bfloat16)
    part = jnp.dot(activated, out_weight, preferred_element_type=jnp.float32).astype(jnp.bfloat16)
    sliced = (CHAIN_CHUNKS, tokens // CHAIN_CHUNKS, width)
    encoded = sum_over_mp(part.reshape(sliced), raw.reshape(sliced), n_mp).reshape(tokens, width)

    keys = jnp.dot(encoded, key_weight, preferred_element_type=jnp.float32).astype(jnp.bfloat16)
    values = jnp.dot(encoded, value_weight, preferred_element_type=jnp.float32).astype(
        jnp.bfloat16
    )
    context, d_queries, d_keys, d_values = attend(queries, keys, values, d_context, spans)

    back = (matmul(d_keys, key_weight, 1, 1) + matmul(d_values, value_weight, 1, 1)).astype(
        jnp.bfloat16
    )
    chunked = (n_dp, width // n_dp, -1)
    key_terms = matmul(encoded, d_keys, 0, 0).astype(jnp.bfloat16).reshape(chunked)
    value_terms = matmul(encoded, d_values, 0, 0).astype(jnp.bfloat16).reshape(chunked)
    d_encoded, grad_key, grad_value = back_sums(
        back.reshape(sliced), key_terms, value_terms, n_mp, n_dp
    )
    d_encoded = d_encoded.reshape(tokens, width)

    d_act = matmul(d_encoded, out_weight, 1, 1)
    d_pre = (d_act * gelu_slope(hidden_pre)).astype(jnp.bfloat16)
    in_terms = matmul(normed, d_pre, 0, 0).astype(jnp.bfloat16).reshape(chunked)
    out_terms = matmul(d_encoded, activated, 0, 0).astype(jnp.bfloat16).reshape(chunked)
    grad_in, grad_out_t = grad_sums(in_terms, out_terms, n_dp)
    return (
        context,
        d_queries,
        jnp.stack([grad_key, grad_value], axis=1),
        grad_in,
        grad_out_t.T,
    )


def solution(mesh):
    placed = (
        P("dp", "mp"),
        P(None, "dp", None),
        P("dp"),
        P("dp"),
        P(None, "mp"),
        P("mp", None),
        P(None, None, "mp"),
        P("dp", "mp"),
    )
    return jax.shard_map(
        per_device,
        mesh=mesh,
        in_specs=placed,
        out_specs=(P("dp", "mp"), P("dp", "mp"), P("dp", None, "mp"), P("dp", "mp"), P("mp", "dp")),
        check_vma=False,
    )
```

```python
import functools

import jax
import jax.numpy as jnp
from jax import lax
from jax.experimental import pallas as pl
from jax.experimental.pallas import tpu as pltpu
from jax.sharding import PartitionSpec as P

DH = 128
SPAN = 64
NEIGH = 2
TAG_ROWS = 16
LANES = 128
CHAIN_CHUNKS = 16
ROOT_LAG = 4
CHAIN_LAG = 8
CHAIN_WINDOW = 4
HEADS_AT_ONCE = 4
VMEM_BYTES = 24 * 1024 * 1024


GELU_C = 0.7978845608028654
GELU_A = 0.044715
EPSILON = 1e-06

WHOLE = pl.BlockSpec(memory_space=pltpu.VMEM)


def gelu_value(values):
    inner = GELU_C * (values + GELU_A * values * values * values)
    return 0.5 * values * (1.0 + jnp.tanh(inner))


def gelu_slope(values):
    inner = GELU_C * (values + GELU_A * values * values * values)
    tanh_value = jnp.tanh(inner)
    return 0.5 * (1.0 + tanh_value) + 0.5 * values * (1.0 - tanh_value * tanh_value) * GELU_C * (
        1.0 + 3.0 * GELU_A * values * values
    )


def rms_normed(rows):
    wide = rows.astype(jnp.float32)
    mean_square = jnp.mean(wide * wide, axis=-1, keepdims=True)
    return (wide * lax.rsqrt(mean_square + EPSILON)).astype(jnp.bfloat16)


def ring_peer(axis, step):
    size = lax.axis_size(axis)
    return {axis: lax.rem(lax.axis_index(axis) + step, size)}


def flip_partner(bit):
    me = lax.axis_index("dp")
    mine = lax.rem(lax.div(me, 1 << bit), 2)
    return {"dp": me + (1 - 2 * mine) * (1 << bit)}, mine


def greet(peers):
    barrier = pltpu.get_barrier_semaphore()
    for peer in peers:
        pl.semaphore_signal(barrier, inc=1, device_id=peer, device_id_type=pl.DeviceIdType.MESH)
    pl.semaphore_wait(barrier, len(peers))


def remote(src, dst, send_sem, recv_sem, peer):
    return pltpu.make_async_remote_copy(
        src_ref=src,
        dst_ref=dst,
        send_sem=send_sem,
        recv_sem=recv_sem,
        device_id=peer,
        device_id_type=pl.DeviceIdType.MESH,
    )


class ChainOverMp:
    def __init__(self, size, part, raw, out, scratch):
        self.size, self.part, self.raw, self.out = size, part, raw, out
        self.staged, self.landing, self.up_send, self.up_recv, self.out_send, self.out_recv = scratch
        self.me = lax.axis_index("mp")
        self.chunks = part.shape[0]
        self.is_end = jnp.logical_or(self.me == 0, self.me == size - 1)
        self.steps = self.chunks + CHAIN_LAG

    def root(self, chunk):
        return self.size // 2 - 1 + chunk % 2

    def up(self, chunk, toward, source):
        side = 0 if toward > 0 else 1
        return remote(
            source.at[chunk],
            self.landing.at[side, chunk],
            self.up_send.at[chunk],
            self.up_recv.at[side, chunk],
            {"mp": self.me + toward},
        )

    def outward(self, chunk, toward):
        side = 0 if toward > 0 else 1
        return remote(
            self.out.at[chunk],
            self.out.at[chunk],
            self.out_send.at[side, chunk],
            self.out_recv.at[chunk],
            {"mp": self.me + toward},
        )

    def arrived(self, chunk, toward):
        self.up(chunk, toward, self.staged).wait_recv()
        return self.landing[0 if toward > 0 else 1, chunk].astype(jnp.float32)

    def inner_up(self, chunk):
        root = self.root(chunk)
        for toward, here in ((1, self.me < root), (-1, self.me > root)):

            @pl.when(here)
            def _(toward=toward):
                total = self.part[chunk].astype(jnp.float32) + self.arrived(chunk, toward)
                self.staged[chunk] = total.astype(jnp.bfloat16)
                self.up(chunk, toward, self.staged).start()

    def inner_root(self, chunk):
        @pl.when(self.me == self.root(chunk))
        def _():
            total = self.part[chunk].astype(jnp.float32)
            total = total + self.arrived(chunk, 1) + self.arrived(chunk, -1)
            if self.raw is not None:
                total = total + self.raw[chunk].astype(jnp.float32)
            self.out[chunk] = total.astype(jnp.bfloat16)
            self.outward(chunk, 1).start()
            self.outward(chunk, -1).start()

    def inner_down(self, chunk):
        root = self.root(chunk)
        for toward, here in ((-1, self.me < root), (1, self.me > root)):

            @pl.when(here)
            def _(toward=toward):
                self.outward(chunk, toward).wait_recv()
                self.outward(chunk, toward).start()

    def end_up(self, chunk):
        for toward, here in ((1, self.me == 0), (-1, self.me == self.size - 1)):

            @pl.when(here)
            def _(toward=toward):
                if chunk >= CHAIN_WINDOW:
                    self.up(chunk - CHAIN_WINDOW, toward, self.part).wait_send()
                self.up(chunk, toward, self.part).start()

    def step(self, index):
        @pl.when(self.is_end)
        def _():
            if index < self.chunks:
                self.end_up(index)

        @pl.when(jnp.logical_not(self.is_end))
        def _():
            if index < self.chunks:
                self.inner_up(index)
            if 0 <= index - ROOT_LAG < self.chunks:
                self.inner_root(index - ROOT_LAG)
            if index >= CHAIN_LAG:
                self.inner_down(index - CHAIN_LAG)

    def finish(self):
        for toward, here in ((1, self.me == 0), (-1, self.me == self.size - 1)):

            @pl.when(here)
            def _(toward=toward):
                for chunk in range(self.chunks):
                    self.outward(chunk, toward).wait_recv()
                for chunk in range(self.chunks - CHAIN_WINDOW, self.chunks):
                    self.up(chunk, toward, self.part).wait_send()

        @pl.when(jnp.logical_not(self.is_end))
        def _():
            for chunk in range(self.chunks):
                root = self.root(chunk)
                for toward, here in ((1, self.me < root), (-1, self.me > root)):

                    @pl.when(here)
                    def _(toward=toward):
                        self.up(chunk, toward, self.staged).wait_send()
                        self.outward(chunk, -toward).wait_send()

                @pl.when(self.me == root)
                def _():
                    self.outward(chunk, 1).wait_send()
                    self.outward(chunk, -1).wait_send()


class HalvingOverDp:
    def __init__(self, bits, source, out, buffers, sends, recvs):
        self.bits, self.source, self.out, self.buffers = bits, source, out, buffers
        self.sends, self.recvs = sends, recvs
        self.flips = [flip_partner(bit) for bit in bits]
        self.stages = len(bits)

    def held(self, stage, group, low):
        wanted = (low,) + group
        if stage > 0:
            return self.buffers[stage - 1].at[self.slot(wanted)]
        return self.source.at[sum(value * (1 << bit) for value, bit in zip(wanted, self.bits))]

    def slot(self, group):
        return sum((value * (1 << place) for place, value in enumerate(group)), 0)

    def copy(self, stage, group):
        peer, mine = self.flips[stage]
        slot = self.slot(group)
        return remote(
            self.held(stage, group, 1 - mine),
            self.buffers[stage].at[slot],
            self.sends[stage].at[slot],
            self.recvs[stage].at[slot],
            peer,
        )

    def orders(self, stage):
        if stage == self.stages - 1:
            return [()]
        later = self.orders(stage + 1)
        mine = self.flips[stage + 1][1]
        return [(1 - mine,) + group for group in later] + [(mine,) + group for group in later]

    def begin(self):
        for group in self.orders(0):
            self.copy(0, group).start()

    def units(self):
        return [
            functools.partial(self.unit, stage, place)
            for stage in range(self.stages - 1)
            for place in range(len(self.orders(stage)))
        ] + [self.last]

    def unit(self, stage, place):
        mine = self.flips[stage][1]
        orders = self.orders(stage)
        group = orders[place]
        buffer = self.buffers[stage]
        self.copy(stage, group).wait_recv()
        slot = self.slot(group)
        kept = self.held(stage, group, mine)[...].astype(jnp.float32)
        buffer[slot] = (kept + buffer[slot].astype(jnp.float32)).astype(jnp.bfloat16)
        if place < len(orders) // 2:
            self.copy(stage + 1, self.orders(stage + 1)[place]).start()

    def last(self):
        stage = self.stages - 1
        mine = self.flips[stage][1]
        self.copy(stage, ()).wait_recv()
        kept = self.held(stage, (), mine)[...].astype(jnp.float32)
        self.out[...] = kept + self.buffers[stage][0].astype(jnp.float32)

    def finish(self):
        for stage in range(self.stages):
            for group in self.orders(stage):
                self.copy(stage, group).wait_send()


def dp_bits(count):
    total = count.bit_length() - 1
    forward = list(range(total))
    return forward, forward[:1] + forward[:0:-1]


def halving_scratch(count, chunk):
    stages = count.bit_length() - 1
    sizes = [count >> (stage + 1) for stage in range(stages)]
    return (
        [pltpu.VMEM((size,) + chunk, jnp.bfloat16) for size in sizes]
        + [pltpu.SemaphoreType.DMA((size,)) for size in sizes]
        + [pltpu.SemaphoreType.DMA((size,)) for size in sizes]
    )


def halving_of(bits, source, out, scratch):
    stages = len(bits)
    return HalvingOverDp(
        bits, source, out, scratch[:stages], scratch[stages : 2 * stages], scratch[2 * stages :]
    )


def mp_scratch(chunks, rows, width):
    return [
        pltpu.VMEM((chunks, rows, width), jnp.bfloat16),
        pltpu.VMEM((2, chunks, rows, width), jnp.bfloat16),
        pltpu.SemaphoreType.DMA((chunks,)),
        pltpu.SemaphoreType.DMA((2, chunks)),
        pltpu.SemaphoreType.DMA((2, chunks)),
        pltpu.SemaphoreType.DMA((chunks,)),
    ]


def params(collective_id):
    return pltpu.CompilerParams(
        collective_id=collective_id, has_side_effects=True, vmem_limit_bytes=VMEM_BYTES
    )


def mp_peers():
    return [ring_peer("mp", step) for step in range(1, lax.axis_size("mp"))]


def dp_flip_peers(count):
    return [flip_partner(bit)[0] for bit in range(count.bit_length() - 1)]


def route_kernel(n_dp, n_mp, straight, split, pairs, *refs):
    if straight:
        labels, message, whole, out, key_out, value_out, labels_in, landing, whole_landing, *sems = refs
    else:
        labels, message, out, key_out, value_out, labels_in, landing, *sems = refs
    *sems, pairs_here, pairs_sem = sems
    fetch = pltpu.make_async_copy(pairs, pairs_here, pairs_sem)
    fetch.start()
    greet([ring_peer("dp", step) for step in range(1, n_dp)] + mp_peers())
    blocks = out.shape[0]
    me_dp, me_mp = lax.axis_index("dp"), lax.axis_index("mp")

    def exchange(source, target, step, send, recv):
        peer = ring_peer("dp", step)
        return remote(
            source.at[peer["dp"]], target.at[step - 1], send.at[step - 1], recv.at[step - 1], peer
        )

    def parts(step):
        return exchange(message, landing, step, sems[0], sems[1])

    def wholes(step):
        return exchange(whole, whole_landing, step, sems[4], sems[5])

    def marks(step):
        return exchange(labels, labels_in, step, sems[6], sems[7])

    others = range(1, n_dp)
    for step in others:
        marks(step).start()
        parts(step).start()
    if straight:
        for step in others:
            wholes(step).start()

    fetch.wait()

    @pl.loop(0, pairs.shape[0] // 16)
    def _(index):
        rows = pl.ds(pl.multiple_of(index * 16, 16), 16)
        key_out[rows, :] = pairs_here[rows, 0, :]
        value_out[rows, :] = pairs_here[rows, 1, :]

    def tags_of(rows):
        return jnp.concatenate([rows.astype(jnp.float32)[:1]] * (out.shape[2] // LANES), axis=1)

    for step in others:
        marks(step).wait_recv()
        parts(step).wait_recv()
    data_rows = pl.ds(0, split)
    tags = [tags_of(labels[me_dp])] + [tags_of(labels_in[step - 1]) for step in others]

    def place(own, arrived, first, where):
        sources = [own[me_dp, first]] + [arrived[step - 1, first] for step in others]
        sources = [rows.astype(jnp.float32) for rows in sources]
        for block in range(blocks):
            value = jnp.zeros_like(sources[0])
            for tag, rows in zip(tags, sources):
                value = jnp.where(tag == block + 1.0, rows, value)
            out[block, where] = value.astype(jnp.bfloat16)

    mine = pl.ds(pl.multiple_of(straight + me_mp * split, 16), split)
    place(message, landing, data_rows, mine)

    def gather(step):
        return remote(
            out.at[:, mine],
            out.at[:, mine],
            sems[2].at[step - 1],
            sems[3].at[step - 1],
            ring_peer("mp", step),
        )

    for step in range(1, n_mp):
        gather(step).start()
    if straight:
        for step in others:
            wholes(step).wait_recv()
        for first in range(0, straight, 16):
            rows = pl.ds(first, 16)
            place(whole, whole_landing, rows, rows)
    for step in range(1, n_mp):
        gather(step).wait_recv()
    for step in others:
        marks(step).wait_send()
        parts(step).wait_send()
        if straight:
            wholes(step).wait_send()
    for step in range(1, n_mp):
        gather(step).wait_send()


def route(pairs, messages, n_dp, n_mp, blocks, length, straight, split):
    width = messages[1].shape[2]
    half = jax.ShapeDtypeStruct((pairs.shape[0], pairs.shape[2]), jnp.bfloat16)
    return pl.pallas_call(
        functools.partial(route_kernel, n_dp, n_mp, straight, split),
        out_shape=(jax.ShapeDtypeStruct((blocks, length, width), jnp.bfloat16), half, half),
        in_specs=[pl.BlockSpec(memory_space=pltpu.HBM)] + [WHOLE] * len(messages),
        out_specs=(WHOLE,) * 3,
        scratch_shapes=[
            pltpu.VMEM((n_dp - 1,) + message.shape[1:], jnp.bfloat16) for message in messages
        ]
        + [
            pltpu.SemaphoreType.DMA((n_dp - 1,)),
            pltpu.SemaphoreType.DMA((n_dp - 1,)),
            pltpu.SemaphoreType.DMA((n_mp - 1,)),
            pltpu.SemaphoreType.DMA((n_mp - 1,)),
            pltpu.SemaphoreType.DMA((n_dp - 1,)),
            pltpu.SemaphoreType.DMA((n_dp - 1,)),
            pltpu.SemaphoreType.DMA((n_dp - 1,)),
            pltpu.SemaphoreType.DMA((n_dp - 1,)),
            pltpu.VMEM(pairs.shape, jnp.bfloat16),
            pltpu.SemaphoreType.DMA,
        ],
        compiler_params=params(0),
        name="route",
    )(pairs, *messages)


def sum_kernel(n_mp, part, raw, hidden, out, slope, *scratch):
    greet(mp_peers())
    total = ChainOverMp(n_mp, part, raw, out, scratch)
    for index in range(total.steps):
        total.step(index)
        if index < total.chunks:
            slope[index] = gelu_slope(hidden[index])
    total.finish()


def sum_over_mp(part, raw, hidden, n_mp):
    rows, width = part.shape[1:]
    return pl.pallas_call(
        functools.partial(sum_kernel, n_mp),
        out_shape=(
            jax.ShapeDtypeStruct(part.shape, jnp.bfloat16),
            jax.ShapeDtypeStruct(hidden.shape, jnp.float32),
        ),
        in_specs=[WHOLE] * 3,
        out_specs=(WHOLE,) * 2,
        scratch_shapes=mp_scratch(part.shape[0], rows, width),
        compiler_params=params(1),
        name="sum_encoded",
    )(part, raw, hidden)


def interleaved(pair):
    return [unit for both in zip(*(one.units() for one in pair)) for unit in both]


def back_kernel(n_mp, n_dp, part, first, second, out, out_pair, *rest):
    greet(mp_peers() + dp_flip_peers(n_dp))
    chain, rest = rest[:6], rest[6:]
    half = len(rest) // 2
    bits = dp_bits(n_dp)
    total = ChainOverMp(n_mp, part, None, out, chain)
    pair = [
        halving_of(bits[0], first, out_pair.at[:, 0], rest[:half]),
        halving_of(bits[1], second, out_pair.at[:, 1], rest[half:]),
    ]
    for one in pair:
        one.begin()
    units = interleaved(pair)
    for index in range(total.steps):
        total.step(index)
        if index > 1 and units:
            units.pop(0)()
    for unit in units:
        unit()
    total.finish()
    for one in pair:
        one.finish()


def back_sums(part, first, second, n_mp, n_dp):
    rows, width = part.shape[1:]
    chunk = first.shape[1:]
    return pl.pallas_call(
        functools.partial(back_kernel, n_mp, n_dp),
        out_shape=(
            jax.ShapeDtypeStruct(part.shape, jnp.bfloat16),
            jax.ShapeDtypeStruct((chunk[0], 2, chunk[1]), jnp.float32),
        ),
        in_specs=[WHOLE] * 3,
        out_specs=(WHOLE,) * 2,
        scratch_shapes=mp_scratch(part.shape[0], rows, width)
        + halving_scratch(n_dp, chunk)
        + halving_scratch(n_dp, chunk),
        compiler_params=params(2),
        name="sum_back",
    )(part, first, second)


def grads_kernel(n_dp, first, second, out_first, out_second, *rest):
    greet(dp_flip_peers(n_dp))
    half = len(rest) // 2
    bits = dp_bits(n_dp)
    pair = [
        halving_of(bits[0], first, out_first, rest[:half]),
        halving_of(bits[1], second, out_second, rest[half:]),
    ]
    for one in pair:
        one.begin()
    for unit in interleaved(pair):
        unit()
    for one in pair:
        one.finish()


def grad_sums(first, second, n_dp):
    chunk = first.shape[1:]
    return pl.pallas_call(
        functools.partial(grads_kernel, n_dp),
        out_shape=(
            jax.ShapeDtypeStruct(chunk, jnp.float32),
            jax.ShapeDtypeStruct(chunk, jnp.float32),
        ),
        in_specs=[WHOLE] * 2,
        out_specs=(WHOLE,) * 2,
        scratch_shapes=halving_scratch(n_dp, chunk) + halving_scratch(n_dp, chunk),
        compiler_params=params(3),
        name="sum_grads",
    )(first, second)


def matmul(left, right, left_dim, right_dim):
    return lax.dot_general(
        left, right, (((left_dim,), (right_dim,)), ((), ())), preferred_element_type=jnp.float32
    )


def attend_kernel(spans, queries, keys, values, grads, context, d_queries, d_keys, d_values):
    scaling = DH ** (-0.5)
    wide = keys.shape[0] // spans
    units = []
    for span in range(spans):
        for head in range(HEADS_AT_ONCE):
            columns = pl.ds(head * DH, DH)
            units.append(
                ((pl.ds(span * SPAN, SPAN), columns), (pl.ds(span * wide, wide), columns))
            )
    scores = [matmul(queries[own], keys[seen], 1, 1) * scaling for own, seen in units]
    d_probs = [matmul(grads[own], values[seen], 1, 1) for own, seen in units]
    weights = [jnp.exp(one - jnp.max(one, axis=-1, keepdims=True)) for one in scores]
    wides = [one / jnp.sum(one, axis=-1, keepdims=True) for one in weights]
    probs = [one.astype(jnp.bfloat16) for one in wides]
    inners = [jnp.sum(d * p, axis=-1, keepdims=True) for d, p in zip(d_probs, wides)]
    d_scores = [
        (p * (d - inner) * scaling).astype(jnp.bfloat16)
        for p, d, inner in zip(wides, d_probs, inners)
    ]
    for (own, seen), p in zip(units, probs):
        context[own] = matmul(p, values[seen], 1, 0).astype(jnp.bfloat16)
    for (own, seen), d in zip(units, d_scores):
        d_queries[own] = matmul(d, keys[seen], 1, 0).astype(jnp.bfloat16)
    for (own, seen), p in zip(units, probs):
        d_values[seen] = matmul(p, grads[own], 0, 0).astype(jnp.bfloat16)
    for (own, seen), d in zip(units, d_scores):
        d_keys[seen] = matmul(d, queries[own], 0, 0).astype(jnp.bfloat16)


def attend(queries, keys, values, grads, spans):
    rows, columns = queries.shape
    count = keys.shape[0]
    narrow = pl.BlockSpec((rows, DH * HEADS_AT_ONCE), lambda head: (0, head))
    tall = pl.BlockSpec((count, DH * HEADS_AT_ONCE), lambda head: (0, head))
    small = jax.ShapeDtypeStruct((rows, columns), jnp.bfloat16)
    large = jax.ShapeDtypeStruct((count, columns), jnp.bfloat16)
    return pl.pallas_call(
        functools.partial(attend_kernel, spans),
        out_shape=(small, small, large, large),
        grid=(columns // (DH * HEADS_AT_ONCE),),
        in_specs=[narrow, tall, tall, narrow],
        out_specs=(narrow, narrow, tall, tall),
        compiler_params=pltpu.CompilerParams(vmem_limit_bytes=VMEM_BYTES),
        name="attend",
    )(queries, keys, values, grads)


def per_device(queries, neighbours, targets, counts, in_weight, out_weight, kv_weight, d_context):
    length, holding, width = neighbours.shape
    n_dp, n_mp = lax.axis_size("dp"), lax.axis_size("mp")
    spans = queries.shape[0] // SPAN
    blocks = NEIGH * spans
    tokens = blocks * length
    is_live = jnp.arange(holding, dtype=jnp.int32) < counts[0]
    owners = jnp.arange(n_dp, dtype=jnp.int32)
    chosen = jnp.logical_and((targets // blocks)[None, :] == owners[:, None], is_live[None, :])
    tags = jnp.sum(jnp.where(chosen, (targets % blocks)[None, :] + 1, 0), axis=1)
    picks = chosen.astype(jnp.bfloat16)

    def picked(rows):
        return jnp.einsum("oh,thd->otd", picks, rows, preferred_element_type=jnp.float32).astype(
            jnp.bfloat16
        )

    split = max(16, length // (2 * n_mp))
    straight = length - split * n_mp
    own = lax.dynamic_slice_in_dim(
        neighbours, straight + lax.axis_index("mp") * split, split, 0
    )
    tag_rows = jnp.broadcast_to(
        tags.astype(jnp.bfloat16)[:, None, None], (n_dp, TAG_ROWS, LANES)
    )
    messages = [tag_rows, picked(own)]
    if straight:
        messages.append(picked(neighbours[:straight]))
    raw, key_weight, value_weight = route(
        kv_weight, messages, n_dp, n_mp, blocks, length, straight, split
    )
    raw = raw.reshape(tokens, width)

    normed = rms_normed(raw)
    hidden_pre = jnp.dot(normed, in_weight, preferred_element_type=jnp.float32)
    activated = lax.optimization_barrier(gelu_value(hidden_pre).astype(jnp.bfloat16))
    part = jnp.dot(activated, out_weight, preferred_element_type=jnp.float32).astype(jnp.bfloat16)
    sliced = (CHAIN_CHUNKS, tokens // CHAIN_CHUNKS, width)
    encoded, slope = sum_over_mp(
        part.reshape(sliced),
        raw.reshape(sliced),
        hidden_pre.reshape(CHAIN_CHUNKS, tokens // CHAIN_CHUNKS, -1),
        n_mp,
    )
    encoded = encoded.reshape(tokens, width)

    keys = jnp.dot(encoded, key_weight, preferred_element_type=jnp.float32).astype(jnp.bfloat16)
    values = jnp.dot(encoded, value_weight, preferred_element_type=jnp.float32).astype(
        jnp.bfloat16
    )
    context, d_queries, d_keys, d_values = attend(queries, keys, values, d_context, spans)

    back = (matmul(d_keys, key_weight, 1, 1) + matmul(d_values, value_weight, 1, 1)).astype(
        jnp.bfloat16
    )
    chunked = (n_dp, width // n_dp, -1)
    key_terms = matmul(encoded, d_keys, 0, 0).astype(jnp.bfloat16).reshape(chunked)
    value_terms = matmul(encoded, d_values, 0, 0).astype(jnp.bfloat16).reshape(chunked)
    d_encoded, grad_kv = back_sums(
        back.reshape(sliced), key_terms, value_terms, n_mp, n_dp
    )
    d_encoded = d_encoded.reshape(tokens, width)

    d_act = matmul(d_encoded, out_weight, 1, 1)
    d_pre = (d_act * slope.reshape(d_act.shape)).astype(jnp.bfloat16)
    in_terms = matmul(normed, d_pre, 0, 0).astype(jnp.bfloat16).reshape(chunked)
    out_terms = matmul(d_encoded, activated, 0, 0).astype(jnp.bfloat16).reshape(chunked)
    grad_in, grad_out_t = grad_sums(in_terms, out_terms, n_dp)
    return (
        context,
        d_queries,
        grad_kv,
        grad_in,
        grad_out_t.T,
    )


def solution(mesh):
    placed = (
        P("dp", "mp"),
        P(None, "dp", None),
        P("dp"),
        P("dp"),
        P(None, "mp"),
        P("mp", None),
        P(None, None, "mp"),
        P("dp", "mp"),
    )
    return jax.shard_map(
        per_device,
        mesh=mesh,
        in_specs=placed,
        out_specs=(P("dp", "mp"), P("dp", "mp"), P("dp", None, "mp"), P("dp", "mp"), P("mp", "dp")),
        check_vma=False,
    )
```

```python
import functools

import jax
import jax.numpy as jnp
from jax import lax
from jax.experimental import pallas as pl
from jax.experimental.pallas import tpu as pltpu
from jax.sharding import PartitionSpec as P

DH = 128
SPAN = 64
NEIGH = 2
TAG_ROWS = 16
LANES = 128
CHAIN_CHUNKS = 32
ROOT_LAG = 6
CHAIN_LAG = 12
CHAIN_WINDOW = 8
HEADS_AT_ONCE = 4
VMEM_BYTES = 24 * 1024 * 1024


GELU_C = 0.7978845608028654
GELU_A = 0.044715
EPSILON = 1e-06

WHOLE = pl.BlockSpec(memory_space=pltpu.VMEM)


def gelu_value(values):
    inner = GELU_C * (values + GELU_A * values * values * values)
    return 0.5 * values * (1.0 + jnp.tanh(inner))


def gelu_slope(values):
    inner = GELU_C * (values + GELU_A * values * values * values)
    tanh_value = jnp.tanh(inner)
    return 0.5 * (1.0 + tanh_value) + 0.5 * values * (1.0 - tanh_value * tanh_value) * GELU_C * (
        1.0 + 3.0 * GELU_A * values * values
    )


def rms_normed(rows):
    wide = rows.astype(jnp.float32)
    mean_square = jnp.mean(wide * wide, axis=-1, keepdims=True)
    return (wide * lax.rsqrt(mean_square + EPSILON)).astype(jnp.bfloat16)


def ring_peer(axis, step):
    size = lax.axis_size(axis)
    return {axis: lax.rem(lax.axis_index(axis) + step, size)}


def flip_partner(bit):
    me = lax.axis_index("dp")
    mine = lax.rem(lax.div(me, 1 << bit), 2)
    return {"dp": me + (1 - 2 * mine) * (1 << bit)}, mine


def greet(peers):
    barrier = pltpu.get_barrier_semaphore()
    for peer in peers:
        pl.semaphore_signal(barrier, inc=1, device_id=peer, device_id_type=pl.DeviceIdType.MESH)
    pl.semaphore_wait(barrier, len(peers))


def remote(src, dst, send_sem, recv_sem, peer):
    return pltpu.make_async_remote_copy(
        src_ref=src,
        dst_ref=dst,
        send_sem=send_sem,
        recv_sem=recv_sem,
        device_id=peer,
        device_id_type=pl.DeviceIdType.MESH,
    )


class ChainOverMp:
    def __init__(self, size, part, raw, out, scratch):
        self.size, self.part, self.raw, self.out = size, part, raw, out
        self.staged, self.landing, self.up_send, self.up_recv, self.out_send, self.out_recv = scratch
        self.me = lax.axis_index("mp")
        self.chunks = part.shape[0]
        self.is_end = jnp.logical_or(self.me == 0, self.me == size - 1)
        self.steps = self.chunks + CHAIN_LAG

    def root(self, chunk):
        return self.size // 2 - 1 + chunk % 2

    def up(self, chunk, toward, source):
        side = 0 if toward > 0 else 1
        return remote(
            source.at[chunk],
            self.landing.at[side, chunk],
            self.up_send.at[chunk],
            self.up_recv.at[side, chunk],
            {"mp": self.me + toward},
        )

    def outward(self, chunk, toward):
        side = 0 if toward > 0 else 1
        return remote(
            self.out.at[chunk],
            self.out.at[chunk],
            self.out_send.at[side, chunk],
            self.out_recv.at[chunk],
            {"mp": self.me + toward},
        )

    def arrived(self, chunk, toward):
        self.up(chunk, toward, self.staged).wait_recv()
        return self.landing[0 if toward > 0 else 1, chunk].astype(jnp.float32)

    def inner_up(self, chunk):
        root = self.root(chunk)
        for toward, here in ((1, self.me < root), (-1, self.me > root)):

            @pl.when(here)
            def _(toward=toward):
                total = self.part[chunk].astype(jnp.float32) + self.arrived(chunk, toward)
                self.staged[chunk] = total.astype(jnp.bfloat16)
                self.up(chunk, toward, self.staged).start()

    def inner_root(self, chunk):
        @pl.when(self.me == self.root(chunk))
        def _():
            total = self.part[chunk].astype(jnp.float32)
            total = total + self.arrived(chunk, 1) + self.arrived(chunk, -1)
            if self.raw is not None:
                total = total + self.raw[chunk].astype(jnp.float32)
            self.out[chunk] = total.astype(jnp.bfloat16)
            self.outward(chunk, 1).start()
            self.outward(chunk, -1).start()

    def inner_down(self, chunk):
        root = self.root(chunk)
        for toward, here in ((-1, self.me < root), (1, self.me > root)):

            @pl.when(here)
            def _(toward=toward):
                self.outward(chunk, toward).wait_recv()
                self.outward(chunk, toward).start()

    def end_up(self, chunk):
        for toward, here in ((1, self.me == 0), (-1, self.me == self.size - 1)):

            @pl.when(here)
            def _(toward=toward):
                if chunk >= CHAIN_WINDOW:
                    self.up(chunk - CHAIN_WINDOW, toward, self.part).wait_send()
                self.up(chunk, toward, self.part).start()

    def step(self, index):
        @pl.when(self.is_end)
        def _():
            if index < self.chunks:
                self.end_up(index)

        @pl.when(jnp.logical_not(self.is_end))
        def _():
            if index < self.chunks:
                self.inner_up(index)
            if 0 <= index - ROOT_LAG < self.chunks:
                self.inner_root(index - ROOT_LAG)
            if index >= CHAIN_LAG:
                self.inner_down(index - CHAIN_LAG)

    def finish(self):
        for toward, here in ((1, self.me == 0), (-1, self.me == self.size - 1)):

            @pl.when(here)
            def _(toward=toward):
                for chunk in range(self.chunks):
                    self.outward(chunk, toward).wait_recv()
                for chunk in range(self.chunks - CHAIN_WINDOW, self.chunks):
                    self.up(chunk, toward, self.part).wait_send()

        @pl.when(jnp.logical_not(self.is_end))
        def _():
            for chunk in range(self.chunks):
                root = self.root(chunk)
                for toward, here in ((1, self.me < root), (-1, self.me > root)):

                    @pl.when(here)
                    def _(toward=toward):
                        self.up(chunk, toward, self.staged).wait_send()
                        self.outward(chunk, -toward).wait_send()

                @pl.when(self.me == root)
                def _():
                    self.outward(chunk, 1).wait_send()
                    self.outward(chunk, -1).wait_send()


class HalvingOverDp:
    def __init__(self, bits, source, out, buffers, sends, recvs):
        self.bits, self.source, self.out, self.buffers = bits, source, out, buffers
        self.sends, self.recvs = sends, recvs
        self.flips = [flip_partner(bit) for bit in bits]
        self.stages = len(bits)

    def held(self, stage, group, low):
        wanted = (low,) + group
        if stage > 0:
            return self.buffers[stage - 1].at[self.slot(wanted)]
        return self.source.at[sum(value * (1 << bit) for value, bit in zip(wanted, self.bits))]

    def slot(self, group):
        return sum((value * (1 << place) for place, value in enumerate(group)), 0)

    def copy(self, stage, group):
        peer, mine = self.flips[stage]
        slot = self.slot(group)
        return remote(
            self.held(stage, group, 1 - mine),
            self.buffers[stage].at[slot],
            self.sends[stage].at[slot],
            self.recvs[stage].at[slot],
            peer,
        )

    def orders(self, stage):
        if stage == self.stages - 1:
            return [()]
        later = self.orders(stage + 1)
        mine = self.flips[stage + 1][1]
        return [(1 - mine,) + group for group in later] + [(mine,) + group for group in later]

    def begin(self):
        for group in self.orders(0):
            self.copy(0, group).start()

    def units(self):
        return [
            functools.partial(self.unit, stage, place)
            for stage in range(self.stages - 1)
            for place in range(len(self.orders(stage)))
        ] + [self.last]

    def unit(self, stage, place):
        mine = self.flips[stage][1]
        orders = self.orders(stage)
        group = orders[place]
        buffer = self.buffers[stage]
        self.copy(stage, group).wait_recv()
        slot = self.slot(group)
        kept = self.held(stage, group, mine)[...].astype(jnp.float32)
        buffer[slot] = (kept + buffer[slot].astype(jnp.float32)).astype(jnp.bfloat16)
        if place < len(orders) // 2:
            self.copy(stage + 1, self.orders(stage + 1)[place]).start()

    def last(self):
        stage = self.stages - 1
        mine = self.flips[stage][1]
        self.copy(stage, ()).wait_recv()
        kept = self.held(stage, (), mine)[...].astype(jnp.float32)
        self.out[...] = kept + self.buffers[stage][0].astype(jnp.float32)

    def finish(self):
        for stage in range(self.stages):
            for group in self.orders(stage):
                self.copy(stage, group).wait_send()


def dp_bits(count):
    total = count.bit_length() - 1
    forward = list(range(total))
    return forward, forward[:1] + forward[:0:-1]


def halving_scratch(count, chunk):
    stages = count.bit_length() - 1
    sizes = [count >> (stage + 1) for stage in range(stages)]
    return (
        [pltpu.VMEM((size,) + chunk, jnp.bfloat16) for size in sizes]
        + [pltpu.SemaphoreType.DMA((size,)) for size in sizes]
        + [pltpu.SemaphoreType.DMA((size,)) for size in sizes]
    )


def halving_of(bits, source, out, scratch):
    stages = len(bits)
    return HalvingOverDp(
        bits, source, out, scratch[:stages], scratch[stages : 2 * stages], scratch[2 * stages :]
    )


def mp_scratch(chunks, rows, width):
    return [
        pltpu.VMEM((chunks, rows, width), jnp.bfloat16),
        pltpu.VMEM((2, chunks, rows, width), jnp.bfloat16),
        pltpu.SemaphoreType.DMA((chunks,)),
        pltpu.SemaphoreType.DMA((2, chunks)),
        pltpu.SemaphoreType.DMA((2, chunks)),
        pltpu.SemaphoreType.DMA((chunks,)),
    ]


def params(collective_id):
    return pltpu.CompilerParams(
        collective_id=collective_id, has_side_effects=True, vmem_limit_bytes=VMEM_BYTES
    )


def mp_peers():
    return [ring_peer("mp", step) for step in range(1, lax.axis_size("mp"))]


def dp_flip_peers(count):
    return [flip_partner(bit)[0] for bit in range(count.bit_length() - 1)]


def route_kernel(n_dp, n_mp, straight, split, pairs, *refs):
    if straight:
        labels, message, whole, out, key_out, value_out, labels_in, landing, whole_landing, *sems = refs
    else:
        labels, message, out, key_out, value_out, labels_in, landing, *sems = refs
    *sems, pairs_here, pairs_sem = sems
    fetch = pltpu.make_async_copy(pairs, pairs_here, pairs_sem)
    fetch.start()
    greet([ring_peer("dp", step) for step in range(1, n_dp)] + mp_peers())
    blocks = out.shape[0]
    me_dp, me_mp = lax.axis_index("dp"), lax.axis_index("mp")

    def exchange(source, target, step, send, recv):
        peer = ring_peer("dp", step)
        return remote(
            source.at[peer["dp"]], target.at[step - 1], send.at[step - 1], recv.at[step - 1], peer
        )

    def parts(step):
        return exchange(message, landing, step, sems[0], sems[1])

    def wholes(step):
        return exchange(whole, whole_landing, step, sems[4], sems[5])

    def marks(step):
        return exchange(labels, labels_in, step, sems[6], sems[7])

    others = range(1, n_dp)
    for step in others:
        marks(step).start()
        parts(step).start()
    if straight:
        for step in others:
            wholes(step).start()

    def tags_of(rows):
        return jnp.concatenate([rows.astype(jnp.float32)[:1]] * (out.shape[2] // LANES), axis=1)

    for step in others:
        marks(step).wait_recv()
        parts(step).wait_recv()
    data_rows = pl.ds(0, split)
    tags = [tags_of(labels[me_dp])] + [tags_of(labels_in[step - 1]) for step in others]

    def place(own, arrived, first, where):
        sources = [own[me_dp, first]] + [arrived[step - 1, first] for step in others]
        sources = [rows.astype(jnp.float32) for rows in sources]
        for block in range(blocks):
            value = jnp.zeros_like(sources[0])
            for tag, rows in zip(tags, sources):
                value = jnp.where(tag == block + 1.0, rows, value)
            out[block, where] = value.astype(jnp.bfloat16)

    mine = pl.ds(pl.multiple_of(straight + me_mp * split, 16), split)
    place(message, landing, data_rows, mine)

    def gather(step):
        return remote(
            out.at[:, mine],
            out.at[:, mine],
            sems[2].at[step - 1],
            sems[3].at[step - 1],
            ring_peer("mp", step),
        )

    for step in range(1, n_mp):
        gather(step).start()
    fetch.wait()

    @pl.loop(0, pairs.shape[0] // 16)
    def _(index):
        rows = pl.ds(pl.multiple_of(index * 16, 16), 16)
        key_out[rows, :] = pairs_here[rows, 0, :]
        value_out[rows, :] = pairs_here[rows, 1, :]

    if straight:
        for step in others:
            wholes(step).wait_recv()
        for first in range(0, straight, 16):
            rows = pl.ds(first, 16)
            place(whole, whole_landing, rows, rows)
    for step in range(1, n_mp):
        gather(step).wait_recv()
    for step in others:
        marks(step).wait_send()
        parts(step).wait_send()
        if straight:
            wholes(step).wait_send()
    for step in range(1, n_mp):
        gather(step).wait_send()


def route(pairs, messages, n_dp, n_mp, blocks, length, straight, split):
    width = messages[1].shape[2]
    half = jax.ShapeDtypeStruct((pairs.shape[0], pairs.shape[2]), jnp.bfloat16)
    return pl.pallas_call(
        functools.partial(route_kernel, n_dp, n_mp, straight, split),
        out_shape=(jax.ShapeDtypeStruct((blocks, length, width), jnp.bfloat16), half, half),
        in_specs=[pl.BlockSpec(memory_space=pltpu.HBM)] + [WHOLE] * len(messages),
        out_specs=(WHOLE,) * 3,
        scratch_shapes=[
            pltpu.VMEM((n_dp - 1,) + message.shape[1:], jnp.bfloat16) for message in messages
        ]
        + [
            pltpu.SemaphoreType.DMA((n_dp - 1,)),
            pltpu.SemaphoreType.DMA((n_dp - 1,)),
            pltpu.SemaphoreType.DMA((n_mp - 1,)),
            pltpu.SemaphoreType.DMA((n_mp - 1,)),
            pltpu.SemaphoreType.DMA((n_dp - 1,)),
            pltpu.SemaphoreType.DMA((n_dp - 1,)),
            pltpu.SemaphoreType.DMA((n_dp - 1,)),
            pltpu.SemaphoreType.DMA((n_dp - 1,)),
            pltpu.VMEM(pairs.shape, jnp.bfloat16),
            pltpu.SemaphoreType.DMA,
        ],
        compiler_params=params(0),
        name="route",
    )(pairs, *messages)


def sum_kernel(n_mp, part, raw, hidden, out, slope, *scratch):
    greet(mp_peers())
    total = ChainOverMp(n_mp, part, raw, out, scratch)
    for index in range(total.steps):
        total.step(index)
        if index < total.chunks:
            slope[index] = gelu_slope(hidden[index])
    total.finish()


def sum_over_mp(part, raw, hidden, n_mp):
    rows, width = part.shape[1:]
    return pl.pallas_call(
        functools.partial(sum_kernel, n_mp),
        out_shape=(
            jax.ShapeDtypeStruct(part.shape, jnp.bfloat16),
            jax.ShapeDtypeStruct(hidden.shape, jnp.float32),
        ),
        in_specs=[WHOLE] * 3,
        out_specs=(WHOLE,) * 2,
        scratch_shapes=mp_scratch(part.shape[0], rows, width),
        compiler_params=params(1),
        name="sum_encoded",
    )(part, raw, hidden)


def interleaved(pair):
    return [unit for both in zip(*(one.units() for one in pair)) for unit in both]


def back_kernel(n_mp, n_dp, part, first, second, out, out_pair, *rest):
    greet(mp_peers() + dp_flip_peers(n_dp))
    chain, rest = rest[:6], rest[6:]
    half = len(rest) // 2
    bits = dp_bits(n_dp)
    total = ChainOverMp(n_mp, part, None, out, chain)
    pair = [
        halving_of(bits[0], first, out_pair.at[:, 0], rest[:half]),
        halving_of(bits[1], second, out_pair.at[:, 1], rest[half:]),
    ]
    for one in pair:
        one.begin()
    units = interleaved(pair)
    for index in range(total.steps):
        total.step(index)
        if index > 1 and units:
            units.pop(0)()
    for unit in units:
        unit()
    total.finish()
    for one in pair:
        one.finish()


def back_sums(part, first, second, n_mp, n_dp):
    rows, width = part.shape[1:]
    chunk = first.shape[1:]
    return pl.pallas_call(
        functools.partial(back_kernel, n_mp, n_dp),
        out_shape=(
            jax.ShapeDtypeStruct(part.shape, jnp.bfloat16),
            jax.ShapeDtypeStruct((chunk[0], 2, chunk[1]), jnp.float32),
        ),
        in_specs=[WHOLE] * 3,
        out_specs=(WHOLE,) * 2,
        scratch_shapes=mp_scratch(part.shape[0], rows, width)
        + halving_scratch(n_dp, chunk)
        + halving_scratch(n_dp, chunk),
        compiler_params=params(2),
        name="sum_back",
    )(part, first, second)


def grads_kernel(n_dp, first, second, out_first, out_second, *rest):
    greet(dp_flip_peers(n_dp))
    half = len(rest) // 2
    bits = dp_bits(n_dp)
    pair = [
        halving_of(bits[0], first, out_first, rest[:half]),
        halving_of(bits[1], second, out_second, rest[half:]),
    ]
    for one in pair:
        one.begin()
    for unit in interleaved(pair):
        unit()
    for one in pair:
        one.finish()


def grad_sums(first, second, n_dp):
    chunk = first.shape[1:]
    return pl.pallas_call(
        functools.partial(grads_kernel, n_dp),
        out_shape=(
            jax.ShapeDtypeStruct(chunk, jnp.float32),
            jax.ShapeDtypeStruct(chunk, jnp.float32),
        ),
        in_specs=[WHOLE] * 2,
        out_specs=(WHOLE,) * 2,
        scratch_shapes=halving_scratch(n_dp, chunk) + halving_scratch(n_dp, chunk),
        compiler_params=params(3),
        name="sum_grads",
    )(first, second)


def matmul(left, right, left_dim, right_dim):
    return lax.dot_general(
        left, right, (((left_dim,), (right_dim,)), ((), ())), preferred_element_type=jnp.float32
    )


def attend_kernel(spans, queries, keys, values, grads, context, d_queries, d_keys, d_values):
    scaling = DH ** (-0.5)
    wide = keys.shape[0] // spans
    units = []
    for span in range(spans):
        for head in range(HEADS_AT_ONCE):
            columns = pl.ds(head * DH, DH)
            units.append(
                ((pl.ds(span * SPAN, SPAN), columns), (pl.ds(span * wide, wide), columns))
            )
    scores = [matmul(queries[own], keys[seen], 1, 1) * scaling for own, seen in units]
    d_probs = [matmul(grads[own], values[seen], 1, 1) for own, seen in units]
    weights = [jnp.exp(one - jnp.max(one, axis=-1, keepdims=True)) for one in scores]
    wides = [one / jnp.sum(one, axis=-1, keepdims=True) for one in weights]
    probs = [one.astype(jnp.bfloat16) for one in wides]
    inners = [jnp.sum(d * p, axis=-1, keepdims=True) for d, p in zip(d_probs, wides)]
    d_scores = [
        (p * (d - inner) * scaling).astype(jnp.bfloat16)
        for p, d, inner in zip(wides, d_probs, inners)
    ]
    for (own, seen), p in zip(units, probs):
        context[own] = matmul(p, values[seen], 1, 0).astype(jnp.bfloat16)
    for (own, seen), d in zip(units, d_scores):
        d_queries[own] = matmul(d, keys[seen], 1, 0).astype(jnp.bfloat16)
    for (own, seen), p in zip(units, probs):
        d_values[seen] = matmul(p, grads[own], 0, 0).astype(jnp.bfloat16)
    for (own, seen), d in zip(units, d_scores):
        d_keys[seen] = matmul(d, queries[own], 0, 0).astype(jnp.bfloat16)


def attend(queries, keys, values, grads, spans):
    rows, columns = queries.shape
    count = keys.shape[0]
    narrow = pl.BlockSpec((rows, DH * HEADS_AT_ONCE), lambda head: (0, head))
    tall = pl.BlockSpec((count, DH * HEADS_AT_ONCE), lambda head: (0, head))
    small = jax.ShapeDtypeStruct((rows, columns), jnp.bfloat16)
    large = jax.ShapeDtypeStruct((count, columns), jnp.bfloat16)
    return pl.pallas_call(
        functools.partial(attend_kernel, spans),
        out_shape=(small, small, large, large),
        grid=(columns // (DH * HEADS_AT_ONCE),),
        in_specs=[narrow, tall, tall, narrow],
        out_specs=(narrow, narrow, tall, tall),
        compiler_params=pltpu.CompilerParams(vmem_limit_bytes=VMEM_BYTES),
        name="attend",
    )(queries, keys, values, grads)


def per_device(queries, neighbours, targets, counts, in_weight, out_weight, kv_weight, d_context):
    length, holding, width = neighbours.shape
    n_dp, n_mp = lax.axis_size("dp"), lax.axis_size("mp")
    spans = queries.shape[0] // SPAN
    blocks = NEIGH * spans
    tokens = blocks * length
    is_live = jnp.arange(holding, dtype=jnp.int32) < counts[0]
    owners = jnp.arange(n_dp, dtype=jnp.int32)
    chosen = jnp.logical_and((targets // blocks)[None, :] == owners[:, None], is_live[None, :])
    tags = jnp.sum(jnp.where(chosen, (targets % blocks)[None, :] + 1, 0), axis=1)
    picks = chosen.astype(jnp.bfloat16)

    def picked(rows):
        return jnp.einsum("oh,thd->otd", picks, rows, preferred_element_type=jnp.float32).astype(
            jnp.bfloat16
        )

    split = max(16, length // (2 * n_mp))
    straight = length - split * n_mp
    own = lax.dynamic_slice_in_dim(
        neighbours, straight + lax.axis_index("mp") * split, split, 0
    )
    tag_rows = jnp.broadcast_to(
        tags.astype(jnp.bfloat16)[:, None, None], (n_dp, TAG_ROWS, LANES)
    )
    messages = [tag_rows, picked(own)]
    if straight:
        messages.append(picked(neighbours[:straight]))
    raw, key_weight, value_weight = route(
        kv_weight, messages, n_dp, n_mp, blocks, length, straight, split
    )
    raw = raw.reshape(tokens, width)

    normed = rms_normed(raw)
    hidden_pre = jnp.dot(normed, in_weight, preferred_element_type=jnp.float32)
    activated = lax.optimization_barrier(gelu_value(hidden_pre).astype(jnp.bfloat16))
    part = jnp.dot(activated, out_weight, preferred_element_type=jnp.float32).astype(jnp.bfloat16)
    sliced = (CHAIN_CHUNKS, tokens // CHAIN_CHUNKS, width)
    encoded, slope = sum_over_mp(
        part.reshape(sliced),
        raw.reshape(sliced),
        hidden_pre.reshape(CHAIN_CHUNKS, tokens // CHAIN_CHUNKS, -1),
        n_mp,
    )
    encoded = encoded.reshape(tokens, width)

    keys = jnp.dot(encoded, key_weight, preferred_element_type=jnp.float32).astype(jnp.bfloat16)
    values = jnp.dot(encoded, value_weight, preferred_element_type=jnp.float32).astype(
        jnp.bfloat16
    )
    context, d_queries, d_keys, d_values = attend(queries, keys, values, d_context, spans)

    back = (matmul(d_keys, key_weight, 1, 1) + matmul(d_values, value_weight, 1, 1)).astype(
        jnp.bfloat16
    )
    chunked = (n_dp, width // n_dp, -1)
    key_terms = matmul(encoded, d_keys, 0, 0).astype(jnp.bfloat16).reshape(chunked)
    value_terms = matmul(encoded, d_values, 0, 0).astype(jnp.bfloat16).reshape(chunked)
    d_encoded, grad_kv = back_sums(
        back.reshape(sliced), key_terms, value_terms, n_mp, n_dp
    )
    d_encoded = d_encoded.reshape(tokens, width)

    d_act = matmul(d_encoded, out_weight, 1, 1)
    d_pre = (d_act * slope.reshape(d_act.shape)).astype(jnp.bfloat16)
    in_terms = matmul(normed, d_pre, 0, 0).astype(jnp.bfloat16).reshape(chunked)
    out_terms = matmul(d_encoded, activated, 0, 0).astype(jnp.bfloat16).reshape(chunked)
    grad_in, grad_out_t = grad_sums(in_terms, out_terms, n_dp)
    return (
        context,
        d_queries,
        grad_kv,
        grad_in,
        grad_out_t.T,
    )


def solution(mesh):
    placed = (
        P("dp", "mp"),
        P(None, "dp", None),
        P("dp"),
        P("dp"),
        P(None, "mp"),
        P("mp", None),
        P(None, None, "mp"),
        P("dp", "mp"),
    )
    return jax.shard_map(
        per_device,
        mesh=mesh,
        in_specs=placed,
        out_specs=(P("dp", "mp"), P("dp", "mp"), P("dp", None, "mp"), P("dp", "mp"), P("mp", "dp")),
        check_vma=False,
    )
```

```python
import functools

import jax
import jax.numpy as jnp
from jax import lax
from jax.experimental import pallas as pl
from jax.experimental.pallas import tpu as pltpu
from jax.sharding import PartitionSpec as P

DH = 128
SPAN = 64
NEIGH = 2
TAG_ROWS = 16
LANES = 128
ENCODED_CHUNKS = 32
BACK_CHUNKS = 16
HEADS_AT_ONCE = 4
VMEM_BYTES = 24 * 1024 * 1024


GELU_C = 0.7978845608028654
GELU_A = 0.044715
EPSILON = 1e-06

WHOLE = pl.BlockSpec(memory_space=pltpu.VMEM)


def gelu_value(values):
    inner = GELU_C * (values + GELU_A * values * values * values)
    return 0.5 * values * (1.0 + jnp.tanh(inner))


def gelu_slope(values):
    inner = GELU_C * (values + GELU_A * values * values * values)
    tanh_value = jnp.tanh(inner)
    return 0.5 * (1.0 + tanh_value) + 0.5 * values * (1.0 - tanh_value * tanh_value) * GELU_C * (
        1.0 + 3.0 * GELU_A * values * values
    )


def rms_normed(rows):
    wide = rows.astype(jnp.float32)
    mean_square = jnp.mean(wide * wide, axis=-1, keepdims=True)
    return (wide * lax.rsqrt(mean_square + EPSILON)).astype(jnp.bfloat16)


def ring_peer(axis, step):
    size = lax.axis_size(axis)
    return {axis: lax.rem(lax.axis_index(axis) + step, size)}


def flip_partner(bit):
    me = lax.axis_index("dp")
    mine = lax.rem(lax.div(me, 1 << bit), 2)
    return {"dp": me + (1 - 2 * mine) * (1 << bit)}, mine


def greet(peers):
    barrier = pltpu.get_barrier_semaphore()
    for peer in peers:
        pl.semaphore_signal(barrier, inc=1, device_id=peer, device_id_type=pl.DeviceIdType.MESH)
    pl.semaphore_wait(barrier, len(peers))


def remote(src, dst, send_sem, recv_sem, peer):
    return pltpu.make_async_remote_copy(
        src_ref=src,
        dst_ref=dst,
        send_sem=send_sem,
        recv_sem=recv_sem,
        device_id=peer,
        device_id_type=pl.DeviceIdType.MESH,
    )


class ChainOverMp:
    def __init__(self, size, part, raw, out, scratch):
        self.size, self.part, self.raw, self.out = size, part, raw, out
        self.staged, self.landing, self.up_send, self.up_recv, self.out_send, self.out_recv = scratch
        self.me = lax.axis_index("mp")
        self.chunks = part.shape[0]
        self.is_end = jnp.logical_or(self.me == 0, self.me == size - 1)
        self.root_lag = 2 + self.chunks // 8
        self.lag = 2 * self.root_lag
        self.window = self.chunks // 4
        self.steps = self.chunks + self.lag

    def root(self, chunk):
        return self.size // 2 - 1 + chunk % 2

    def up(self, chunk, toward, source):
        side = 0 if toward > 0 else 1
        return remote(
            source.at[chunk],
            self.landing.at[side, chunk],
            self.up_send.at[chunk],
            self.up_recv.at[side, chunk],
            {"mp": self.me + toward},
        )

    def outward(self, chunk, toward):
        side = 0 if toward > 0 else 1
        return remote(
            self.out.at[chunk],
            self.out.at[chunk],
            self.out_send.at[side, chunk],
            self.out_recv.at[chunk],
            {"mp": self.me + toward},
        )

    def arrived(self, chunk, toward):
        self.up(chunk, toward, self.staged).wait_recv()
        return self.landing[0 if toward > 0 else 1, chunk].astype(jnp.float32)

    def inner_up(self, chunk):
        root = self.root(chunk)
        for toward, here in ((1, self.me < root), (-1, self.me > root)):

            @pl.when(here)
            def _(toward=toward):
                total = self.part[chunk].astype(jnp.float32) + self.arrived(chunk, toward)
                self.staged[chunk] = total.astype(jnp.bfloat16)
                self.up(chunk, toward, self.staged).start()

    def inner_root(self, chunk):
        @pl.when(self.me == self.root(chunk))
        def _():
            total = self.part[chunk].astype(jnp.float32)
            total = total + self.arrived(chunk, 1) + self.arrived(chunk, -1)
            if self.raw is not None:
                total = total + self.raw[chunk].astype(jnp.float32)
            self.out[chunk] = total.astype(jnp.bfloat16)
            self.outward(chunk, 1).start()
            self.outward(chunk, -1).start()

    def inner_down(self, chunk):
        root = self.root(chunk)
        for toward, here in ((-1, self.me < root), (1, self.me > root)):

            @pl.when(here)
            def _(toward=toward):
                self.outward(chunk, toward).wait_recv()
                self.outward(chunk, toward).start()

    def end_up(self, chunk):
        for toward, here in ((1, self.me == 0), (-1, self.me == self.size - 1)):

            @pl.when(here)
            def _(toward=toward):
                if chunk >= self.window:
                    self.up(chunk - self.window, toward, self.part).wait_send()
                self.up(chunk, toward, self.part).start()

    def step(self, index):
        @pl.when(self.is_end)
        def _():
            if index < self.chunks:
                self.end_up(index)

        @pl.when(jnp.logical_not(self.is_end))
        def _():
            if index < self.chunks:
                self.inner_up(index)
            if 0 <= index - self.root_lag < self.chunks:
                self.inner_root(index - self.root_lag)
            if index >= self.lag:
                self.inner_down(index - self.lag)

    def finish(self):
        for toward, here in ((1, self.me == 0), (-1, self.me == self.size - 1)):

            @pl.when(here)
            def _(toward=toward):
                for chunk in range(self.chunks):
                    self.outward(chunk, toward).wait_recv()
                for chunk in range(self.chunks - self.window, self.chunks):
                    self.up(chunk, toward, self.part).wait_send()

        @pl.when(jnp.logical_not(self.is_end))
        def _():
            for chunk in range(self.chunks):
                root = self.root(chunk)
                for toward, here in ((1, self.me < root), (-1, self.me > root)):

                    @pl.when(here)
                    def _(toward=toward):
                        self.up(chunk, toward, self.staged).wait_send()
                        self.outward(chunk, -toward).wait_send()

                @pl.when(self.me == root)
                def _():
                    self.outward(chunk, 1).wait_send()
                    self.outward(chunk, -1).wait_send()


class HalvingOverDp:
    def __init__(self, bits, source, out, buffers, sends, recvs):
        self.bits, self.source, self.out, self.buffers = bits, source, out, buffers
        self.sends, self.recvs = sends, recvs
        self.flips = [flip_partner(bit) for bit in bits]
        self.stages = len(bits)

    def held(self, stage, group, low):
        wanted = (low,) + group
        if stage > 0:
            return self.buffers[stage - 1].at[self.slot(wanted)]
        return self.source.at[sum(value * (1 << bit) for value, bit in zip(wanted, self.bits))]

    def slot(self, group):
        return sum((value * (1 << place) for place, value in enumerate(group)), 0)

    def copy(self, stage, group):
        peer, mine = self.flips[stage]
        slot = self.slot(group)
        return remote(
            self.held(stage, group, 1 - mine),
            self.buffers[stage].at[slot],
            self.sends[stage].at[slot],
            self.recvs[stage].at[slot],
            peer,
        )

    def orders(self, stage):
        if stage == self.stages - 1:
            return [()]
        later = self.orders(stage + 1)
        mine = self.flips[stage + 1][1]
        return [(1 - mine,) + group for group in later] + [(mine,) + group for group in later]

    def begin(self):
        for group in self.orders(0):
            self.copy(0, group).start()

    def units(self):
        return [
            functools.partial(self.unit, stage, place)
            for stage in range(self.stages - 1)
            for place in range(len(self.orders(stage)))
        ] + [self.last]

    def unit(self, stage, place):
        mine = self.flips[stage][1]
        orders = self.orders(stage)
        group = orders[place]
        buffer = self.buffers[stage]
        self.copy(stage, group).wait_recv()
        slot = self.slot(group)
        kept = self.held(stage, group, mine)[...].astype(jnp.float32)
        buffer[slot] = (kept + buffer[slot].astype(jnp.float32)).astype(jnp.bfloat16)
        if place < len(orders) // 2:
            self.copy(stage + 1, self.orders(stage + 1)[place]).start()

    def last(self):
        stage = self.stages - 1
        mine = self.flips[stage][1]
        self.copy(stage, ()).wait_recv()
        kept = self.held(stage, (), mine)[...].astype(jnp.float32)
        self.out[...] = kept + self.buffers[stage][0].astype(jnp.float32)

    def finish(self):
        for stage in range(self.stages):
            for group in self.orders(stage):
                self.copy(stage, group).wait_send()


def dp_bits(count):
    total = count.bit_length() - 1
    forward = list(range(total))
    return forward, forward[:1] + forward[:0:-1]


def halving_scratch(count, chunk):
    stages = count.bit_length() - 1
    sizes = [count >> (stage + 1) for stage in range(stages)]
    return (
        [pltpu.VMEM((size,) + chunk, jnp.bfloat16) for size in sizes]
        + [pltpu.SemaphoreType.DMA((size,)) for size in sizes]
        + [pltpu.SemaphoreType.DMA((size,)) for size in sizes]
    )


def halving_of(bits, source, out, scratch):
    stages = len(bits)
    return HalvingOverDp(
        bits, source, out, scratch[:stages], scratch[stages : 2 * stages], scratch[2 * stages :]
    )


def mp_scratch(chunks, rows, width):
    return [
        pltpu.VMEM((chunks, rows, width), jnp.bfloat16),
        pltpu.VMEM((2, chunks, rows, width), jnp.bfloat16),
        pltpu.SemaphoreType.DMA((chunks,)),
        pltpu.SemaphoreType.DMA((2, chunks)),
        pltpu.SemaphoreType.DMA((2, chunks)),
        pltpu.SemaphoreType.DMA((chunks,)),
    ]


def params(collective_id):
    return pltpu.CompilerParams(
        collective_id=collective_id, has_side_effects=True, vmem_limit_bytes=VMEM_BYTES
    )


def mp_peers():
    return [ring_peer("mp", step) for step in range(1, lax.axis_size("mp"))]


def dp_flip_peers(count):
    return [flip_partner(bit)[0] for bit in range(count.bit_length() - 1)]


def route_kernel(n_dp, n_mp, straight, split, pairs, *refs):
    if straight:
        labels, message, whole, out, key_out, value_out, labels_in, landing, whole_landing, *sems = refs
    else:
        labels, message, out, key_out, value_out, labels_in, landing, *sems = refs
    *sems, pairs_here, pairs_sem = sems
    fetch = pltpu.make_async_copy(pairs, pairs_here, pairs_sem)
    fetch.start()
    greet([ring_peer("dp", step) for step in range(1, n_dp)] + mp_peers())
    blocks = out.shape[0]
    me_dp, me_mp = lax.axis_index("dp"), lax.axis_index("mp")

    def exchange(source, target, step, send, recv):
        peer = ring_peer("dp", step)
        return remote(
            source.at[peer["dp"]], target.at[step - 1], send.at[step - 1], recv.at[step - 1], peer
        )

    def parts(step):
        return exchange(message, landing, step, sems[0], sems[1])

    def wholes(step):
        return exchange(whole, whole_landing, step, sems[4], sems[5])

    def marks(step):
        return exchange(labels, labels_in, step, sems[6], sems[7])

    others = range(1, n_dp)
    for step in others:
        marks(step).start()
        parts(step).start()
    if straight:
        for step in others:
            wholes(step).start()

    def tags_of(rows):
        return jnp.concatenate([rows.astype(jnp.float32)[:1]] * (out.shape[2] // LANES), axis=1)

    for step in others:
        marks(step).wait_recv()
        parts(step).wait_recv()
    data_rows = pl.ds(0, split)
    tags = [tags_of(labels[me_dp])] + [tags_of(labels_in[step - 1]) for step in others]

    def place(own, arrived, first, where):
        sources = [own[me_dp, first]] + [arrived[step - 1, first] for step in others]
        sources = [rows.astype(jnp.float32) for rows in sources]
        for block in range(blocks):
            value = jnp.zeros_like(sources[0])
            for tag, rows in zip(tags, sources):
                value = jnp.where(tag == block + 1.0, rows, value)
            out[block, where] = value.astype(jnp.bfloat16)

    mine = pl.ds(pl.multiple_of(straight + me_mp * split, 16), split)
    place(message, landing, data_rows, mine)

    def gather(step):
        return remote(
            out.at[:, mine],
            out.at[:, mine],
            sems[2].at[step - 1],
            sems[3].at[step - 1],
            ring_peer("mp", step),
        )

    for step in range(1, n_mp):
        gather(step).start()
    fetch.wait()

    @pl.loop(0, pairs.shape[0] // 16)
    def _(index):
        rows = pl.ds(pl.multiple_of(index * 16, 16), 16)
        key_out[rows, :] = pairs_here[rows, 0, :]
        value_out[rows, :] = pairs_here[rows, 1, :]

    if straight:
        for step in others:
            wholes(step).wait_recv()
        for first in range(0, straight, 16):
            rows = pl.ds(first, 16)
            place(whole, whole_landing, rows, rows)
    for step in range(1, n_mp):
        gather(step).wait_recv()
    for step in others:
        marks(step).wait_send()
        parts(step).wait_send()
        if straight:
            wholes(step).wait_send()
    for step in range(1, n_mp):
        gather(step).wait_send()


def route(pairs, messages, n_dp, n_mp, blocks, length, straight, split):
    width = messages[1].shape[2]
    half = jax.ShapeDtypeStruct((pairs.shape[0], pairs.shape[2]), jnp.bfloat16)
    return pl.pallas_call(
        functools.partial(route_kernel, n_dp, n_mp, straight, split),
        out_shape=(jax.ShapeDtypeStruct((blocks, length, width), jnp.bfloat16), half, half),
        in_specs=[pl.BlockSpec(memory_space=pltpu.HBM)] + [WHOLE] * len(messages),
        out_specs=(WHOLE,) * 3,
        scratch_shapes=[
            pltpu.VMEM((n_dp - 1,) + message.shape[1:], jnp.bfloat16) for message in messages
        ]
        + [
            pltpu.SemaphoreType.DMA((n_dp - 1,)),
            pltpu.SemaphoreType.DMA((n_dp - 1,)),
            pltpu.SemaphoreType.DMA((n_mp - 1,)),
            pltpu.SemaphoreType.DMA((n_mp - 1,)),
            pltpu.SemaphoreType.DMA((n_dp - 1,)),
            pltpu.SemaphoreType.DMA((n_dp - 1,)),
            pltpu.SemaphoreType.DMA((n_dp - 1,)),
            pltpu.SemaphoreType.DMA((n_dp - 1,)),
            pltpu.VMEM(pairs.shape, jnp.bfloat16),
            pltpu.SemaphoreType.DMA,
        ],
        compiler_params=params(0),
        name="route",
    )(pairs, *messages)


def sum_kernel(n_mp, part, raw, hidden, out, slope, *scratch):
    greet(mp_peers())
    total = ChainOverMp(n_mp, part, raw, out, scratch)
    for index in range(total.steps):
        total.step(index)
        if index < total.chunks:
            slope[index] = gelu_slope(hidden[index])
    total.finish()


def sum_over_mp(part, raw, hidden, n_mp):
    rows, width = part.shape[1:]
    return pl.pallas_call(
        functools.partial(sum_kernel, n_mp),
        out_shape=(
            jax.ShapeDtypeStruct(part.shape, jnp.bfloat16),
            jax.ShapeDtypeStruct(hidden.shape, jnp.float32),
        ),
        in_specs=[WHOLE] * 3,
        out_specs=(WHOLE,) * 2,
        scratch_shapes=mp_scratch(part.shape[0], rows, width),
        compiler_params=params(1),
        name="sum_encoded",
    )(part, raw, hidden)


def interleaved(pair):
    return [unit for both in zip(*(one.units() for one in pair)) for unit in both]


def back_kernel(n_mp, n_dp, part, first, second, out, out_pair, *rest):
    greet(mp_peers() + dp_flip_peers(n_dp))
    chain, rest = rest[:6], rest[6:]
    half = len(rest) // 2
    bits = dp_bits(n_dp)
    total = ChainOverMp(n_mp, part, None, out, chain)
    pair = [
        halving_of(bits[0], first, out_pair.at[:, 0], rest[:half]),
        halving_of(bits[1], second, out_pair.at[:, 1], rest[half:]),
    ]
    for one in pair:
        one.begin()
    units = interleaved(pair)
    for index in range(total.steps):
        total.step(index)
        if index > 1 and units:
            units.pop(0)()
    for unit in units:
        unit()
    total.finish()
    for one in pair:
        one.finish()


def back_sums(part, first, second, n_mp, n_dp):
    rows, width = part.shape[1:]
    chunk = first.shape[1:]
    return pl.pallas_call(
        functools.partial(back_kernel, n_mp, n_dp),
        out_shape=(
            jax.ShapeDtypeStruct(part.shape, jnp.bfloat16),
            jax.ShapeDtypeStruct((chunk[0], 2, chunk[1]), jnp.float32),
        ),
        in_specs=[WHOLE] * 3,
        out_specs=(WHOLE,) * 2,
        scratch_shapes=mp_scratch(part.shape[0], rows, width)
        + halving_scratch(n_dp, chunk)
        + halving_scratch(n_dp, chunk),
        compiler_params=params(2),
        name="sum_back",
    )(part, first, second)


def grads_kernel(n_dp, first, second, out_first, out_second, *rest):
    greet(dp_flip_peers(n_dp))
    half = len(rest) // 2
    bits = dp_bits(n_dp)
    pair = [
        halving_of(bits[0], first, out_first, rest[:half]),
        halving_of(bits[1], second, out_second, rest[half:]),
    ]
    for one in pair:
        one.begin()
    for unit in interleaved(pair):
        unit()
    for one in pair:
        one.finish()


def grad_sums(first, second, n_dp):
    chunk = first.shape[1:]
    return pl.pallas_call(
        functools.partial(grads_kernel, n_dp),
        out_shape=(
            jax.ShapeDtypeStruct(chunk, jnp.float32),
            jax.ShapeDtypeStruct(chunk, jnp.float32),
        ),
        in_specs=[WHOLE] * 2,
        out_specs=(WHOLE,) * 2,
        scratch_shapes=halving_scratch(n_dp, chunk) + halving_scratch(n_dp, chunk),
        compiler_params=params(3),
        name="sum_grads",
    )(first, second)


def matmul(left, right, left_dim, right_dim):
    return lax.dot_general(
        left, right, (((left_dim,), (right_dim,)), ((), ())), preferred_element_type=jnp.float32
    )


def attend_kernel(spans, queries, keys, values, grads, context, d_queries, d_keys, d_values):
    scaling = DH ** (-0.5)
    wide = keys.shape[0] // spans
    units = []
    for span in range(spans):
        for head in range(HEADS_AT_ONCE):
            columns = pl.ds(head * DH, DH)
            units.append(
                ((pl.ds(span * SPAN, SPAN), columns), (pl.ds(span * wide, wide), columns))
            )
    scores = [matmul(queries[own], keys[seen], 1, 1) * scaling for own, seen in units]
    d_probs = [matmul(grads[own], values[seen], 1, 1) for own, seen in units]
    weights = [jnp.exp(one - jnp.max(one, axis=-1, keepdims=True)) for one in scores]
    wides = [one / jnp.sum(one, axis=-1, keepdims=True) for one in weights]
    probs = [one.astype(jnp.bfloat16) for one in wides]
    inners = [jnp.sum(d * p, axis=-1, keepdims=True) for d, p in zip(d_probs, wides)]
    d_scores = [
        (p * (d - inner) * scaling).astype(jnp.bfloat16)
        for p, d, inner in zip(wides, d_probs, inners)
    ]
    for (own, seen), p in zip(units, probs):
        context[own] = matmul(p, values[seen], 1, 0).astype(jnp.bfloat16)
    for (own, seen), d in zip(units, d_scores):
        d_queries[own] = matmul(d, keys[seen], 1, 0).astype(jnp.bfloat16)
    for (own, seen), p in zip(units, probs):
        d_values[seen] = matmul(p, grads[own], 0, 0).astype(jnp.bfloat16)
    for (own, seen), d in zip(units, d_scores):
        d_keys[seen] = matmul(d, queries[own], 0, 0).astype(jnp.bfloat16)


def attend(queries, keys, values, grads, spans):
    rows, columns = queries.shape
    count = keys.shape[0]
    narrow = pl.BlockSpec((rows, DH * HEADS_AT_ONCE), lambda head: (0, head))
    tall = pl.BlockSpec((count, DH * HEADS_AT_ONCE), lambda head: (0, head))
    small = jax.ShapeDtypeStruct((rows, columns), jnp.bfloat16)
    large = jax.ShapeDtypeStruct((count, columns), jnp.bfloat16)
    return pl.pallas_call(
        functools.partial(attend_kernel, spans),
        out_shape=(small, small, large, large),
        grid=(columns // (DH * HEADS_AT_ONCE),),
        in_specs=[narrow, tall, tall, narrow],
        out_specs=(narrow, narrow, tall, tall),
        compiler_params=pltpu.CompilerParams(vmem_limit_bytes=VMEM_BYTES),
        name="attend",
    )(queries, keys, values, grads)


def per_device(queries, neighbours, targets, counts, in_weight, out_weight, kv_weight, d_context):
    length, holding, width = neighbours.shape
    n_dp, n_mp = lax.axis_size("dp"), lax.axis_size("mp")
    spans = queries.shape[0] // SPAN
    blocks = NEIGH * spans
    tokens = blocks * length
    is_live = jnp.arange(holding, dtype=jnp.int32) < counts[0]
    owners = jnp.arange(n_dp, dtype=jnp.int32)
    chosen = jnp.logical_and((targets // blocks)[None, :] == owners[:, None], is_live[None, :])
    tags = jnp.sum(jnp.where(chosen, (targets % blocks)[None, :] + 1, 0), axis=1)
    picks = chosen.astype(jnp.bfloat16)

    def picked(rows):
        return jnp.einsum("oh,thd->otd", picks, rows, preferred_element_type=jnp.float32).astype(
            jnp.bfloat16
        )

    split = max(16, length // (2 * n_mp))
    straight = length - split * n_mp
    own = lax.dynamic_slice_in_dim(
        neighbours, straight + lax.axis_index("mp") * split, split, 0
    )
    tag_rows = jnp.broadcast_to(
        tags.astype(jnp.bfloat16)[:, None, None], (n_dp, TAG_ROWS, LANES)
    )
    messages = [tag_rows, picked(own)]
    if straight:
        messages.append(picked(neighbours[:straight]))
    raw, key_weight, value_weight = route(
        kv_weight, messages, n_dp, n_mp, blocks, length, straight, split
    )
    raw = raw.reshape(tokens, width)

    normed = rms_normed(raw)
    hidden_pre = jnp.dot(normed, in_weight, preferred_element_type=jnp.float32)
    activated = lax.optimization_barrier(gelu_value(hidden_pre).astype(jnp.bfloat16))
    part = jnp.dot(activated, out_weight, preferred_element_type=jnp.float32).astype(jnp.bfloat16)
    sliced = (ENCODED_CHUNKS, tokens // ENCODED_CHUNKS, width)
    encoded, slope = sum_over_mp(
        part.reshape(sliced),
        raw.reshape(sliced),
        hidden_pre.reshape(ENCODED_CHUNKS, tokens // ENCODED_CHUNKS, -1),
        n_mp,
    )
    encoded = encoded.reshape(tokens, width)

    keys = jnp.dot(encoded, key_weight, preferred_element_type=jnp.float32).astype(jnp.bfloat16)
    values = jnp.dot(encoded, value_weight, preferred_element_type=jnp.float32).astype(
        jnp.bfloat16
    )
    context, d_queries, d_keys, d_values = attend(queries, keys, values, d_context, spans)

    back = (matmul(d_keys, key_weight, 1, 1) + matmul(d_values, value_weight, 1, 1)).astype(
        jnp.bfloat16
    )
    chunked = (n_dp, width // n_dp, -1)
    key_terms = matmul(encoded, d_keys, 0, 0).astype(jnp.bfloat16).reshape(chunked)
    value_terms = matmul(encoded, d_values, 0, 0).astype(jnp.bfloat16).reshape(chunked)
    d_encoded, grad_kv = back_sums(
        back.reshape(BACK_CHUNKS, tokens // BACK_CHUNKS, width), key_terms, value_terms, n_mp, n_dp
    )
    d_encoded = d_encoded.reshape(tokens, width)

    d_act = matmul(d_encoded, out_weight, 1, 1)
    d_pre = (d_act * slope.reshape(d_act.shape)).astype(jnp.bfloat16)
    in_terms = matmul(normed, d_pre, 0, 0).astype(jnp.bfloat16).reshape(chunked)
    out_terms = matmul(d_encoded, activated, 0, 0).astype(jnp.bfloat16).reshape(chunked)
    grad_in, grad_out_t = grad_sums(in_terms, out_terms, n_dp)
    return (
        context,
        d_queries,
        grad_kv,
        grad_in,
        grad_out_t.T,
    )


def solution(mesh):
    placed = (
        P("dp", "mp"),
        P(None, "dp", None),
        P("dp"),
        P("dp"),
        P(None, "mp"),
        P("mp", None),
        P(None, None, "mp"),
        P("dp", "mp"),
    )
    return jax.shard_map(
        per_device,
        mesh=mesh,
        in_specs=placed,
        out_specs=(P("dp", "mp"), P("dp", "mp"), P("dp", None, "mp"), P("dp", "mp"), P("mp", "dp")),
        check_vma=False,
    )
```
